128 devices in a mesh: dp: 4 (over y), seq: 32 (over z, x, core).
Axes of the slice: x: 4, y: 4, z: 4, core: 2. Of those that a mesh axis runs over, the one named last changes fastest.
Arguments:
- tile_rows: bfloat16 [4, 65536, 768], P('dp', 'seq'), may hold values from -6 to 6
- block_dest: int32 [4, 512], P('dp', 'seq'), may hold values from 0 to 31, as said below
- norm_gain: float32 [768], replicated, may hold values from 0.25 to 1.75
- qkv_weight: bfloat16 [768, 2304], replicated, may hold values from -1 to 1
- out_weight: bfloat16 [768, 768], replicated, may hold values from -0.21875 to 0.21875
- cotangent: bfloat16 [4, 65536, 768], P('dp', 'seq'), may hold values from -0.0625 to 0.0625
Outputs:
- encoded: bfloat16 [4, 65536, 768], P('dp', 'seq')
- out_weight_grad: float32 [768, 768], P('seq')
The draws below stay inside these ranges and needn't reach their ends.
Inputs may be any that keep to these rules, and one draw needn't show every extreme that they name: `block_dest`: in each slide every destination shard is named exactly 16 times, and the 16 blocks of one source shard name 16 different destinations, so one destination at most 1 times.
All inputs are finite; a program needn't handle non-finite values.
Results may differ from the reference program's by a relative error of at most 0.022.
The reference program's roundings to bfloat16 on the way (of `inputs`, `normed`, `qkv` and `attn`) count: a program that leaves them out, or rounds other values in their place, can miss the bound.
Values may be sent and summed in bfloat16 or wider, within the bound.
A program may use at most 192 MiB of HBM per device.

```python
import math
import jax
import jax.numpy as jnp
import numpy as np
from jax import lax

D = 768
HEADS = 12
HEAD_DIM = 64
BLK = 128
SEG = 512
RATE = 16
SRC_BLK = 16
BLOCKS = 512
LENGTH = 65536
SLIDES = 4


def draw_block_dest(key, part):
    key = jax.random.fold_in(key, 1)
    shards = BLOCKS // SRC_BLK

    def one_slide(slide_key):
        first_key, second_key = jax.random.split(slide_key)
        offsets = jax.random.permutation(first_key, shards)
        listed = offsets[:SRC_BLK]
        source = jnp.arange(shards)[:, None]
        targets = (source + listed[None, :]) % shards
        row_keys = jax.random.split(second_key, shards)
        shuffled = jax.vmap(lambda row_key, row: jax.random.permutation(row_key, row))(row_keys, targets)
        return shuffled.reshape(-1)
    return jax.vmap(one_slide)(jax.random.split(key, SLIDES)).astype(jnp.int32)


def draw_qkv_weight(key, part):
    key = jax.random.fold_in(key, 2)
    factor = 1.0
    values = jax.random.normal(key, (D, 3 * D), jnp.float32) * (factor / math.sqrt(D))
    return jnp.clip(values, -1.0, 1.0).astype(jnp.bfloat16)


def block_scale(own_key, dims, cuts, low, largest):
    loudness, own = 1.0, jax.random.fold_in(own_key, 6)
    for position, parts in cuts:
        draws = jnp.exp(jax.random.uniform(jax.random.fold_in(own, position), (parts,), jnp.float32, low / len(cuts), largest / len(cuts)))
        loudness = loudness * jnp.repeat(draws, dims[position] // parts).reshape([-1 if axis == position else 1 for axis in range(len(dims))])
    return loudness


def gaussian(own_key, dims, scale, bound, cuts=(), dtype=jnp.bfloat16):
    drawn = scale * jax.random.normal(own_key, dims, jnp.float32)
    if cuts:
        drawn = drawn * block_scale(own_key, dims, cuts, -0.22, 0.18)
    return jnp.clip(drawn, -bound, bound).astype(dtype)


def setup_inputs(seed: int = 0) -> dict:
    key_of = jax.random.split(jax.random.key(seed), 7)
    tile_rows = gaussian(key_of[0], (SLIDES, LENGTH, D), 1.0, 6.0, ((0, 4), (1, 32)))
    block_dest = draw_block_dest(jax.random.fold_in(key_of[6], 71), 0)
    norm_gain = jnp.clip(1.0 + 0.15 * jax.random.normal(key_of[2], (D,), jnp.float32), 0.25, 1.75)
    qkv_weight = draw_qkv_weight(jax.random.fold_in(key_of[6], 71), 0)
    out_weight = gaussian(key_of[4], (D, D), D ** -0.5, 0.21875)
    cotangent = gaussian(key_of[5], (SLIDES, LENGTH, D), 0.004, 0.0625, ((0, 4), (1, 32)))
    return dict(tile_rows=tile_rows, block_dest=block_dest, norm_gain=norm_gain, qkv_weight=qkv_weight, out_weight=out_weight, cotangent=cotangent)


score_scale = 0.125
norm_eps = 1e-06

def normalize(values, norm_gain):
    values = values.astype(jnp.float32)
    center = values - lax.optimization_barrier(jnp.mean(values, axis=-1, keepdims=True))
    spread = lax.optimization_barrier(jnp.mean(center * center, axis=-1, keepdims=True))
    return (center * lax.rsqrt(spread + norm_eps) * norm_gain.astype(jnp.float32)).astype(jnp.bfloat16)

def local_segment(pieces):
    queries, keys_seg, values_seg = pieces
    scores = jnp.einsum('qhd,khd->hqk', queries.astype(jnp.float32), keys_seg.astype(jnp.float32)) * score_scale
    peak = lax.optimization_barrier(jnp.max(scores, axis=-1))
    weights = jnp.exp(scores - peak[..., None])
    total = lax.optimization_barrier(jnp.sum(weights, axis=-1))
    rounded = lax.optimization_barrier(weights.astype(jnp.bfloat16))
    mixed = jnp.einsum('hqk,khd->qhd', rounded.astype(jnp.float32), values_seg.astype(jnp.float32))
    return (mixed / total.T[:, :, None], (peak + jnp.log(total)).T)

def far_head(pieces):
    queries, keys_far, values_far = pieces
    scores = jnp.dot(queries.astype(jnp.float32), keys_far.astype(jnp.float32).T) * score_scale
    peak = lax.optimization_barrier(jnp.max(scores, axis=-1))
    weights = jnp.exp(scores - peak[:, None])
    total = lax.optimization_barrier(jnp.sum(weights, axis=-1))
    rounded = lax.optimization_barrier(weights.astype(jnp.bfloat16))
    mixed = jnp.dot(rounded.astype(jnp.float32), values_far.astype(jnp.float32))
    return (mixed / total[:, None], peak + jnp.log(total))

def reference(tile_rows, block_dest, norm_gain, qkv_weight, out_weight, cotangent):
    residue = np.arange(HEADS) % RATE
    head_ids = np.arange(HEADS)
    far_rows = LENGTH // RATE

    def pick(array):
        return array.reshape(far_rows, RATE, HEADS, HEAD_DIM)[:, residue, head_ids]

    def one_slide(carry, items):
        slide_tiles, slide_dest, slide_grad = items
        blocks = slide_tiles.reshape(BLOCKS, BLK, D)
        order = jnp.argsort(slide_dest, stable=True)
        inputs = blocks[order].reshape(LENGTH, D)
        normed = normalize(inputs, norm_gain)
        qkv = jnp.dot(normed, qkv_weight, preferred_element_type=jnp.float32).astype(jnp.bfloat16)
        queries = qkv[:, :D].reshape(LENGTH, HEADS, HEAD_DIM)
        keys_all = qkv[:, D:2 * D].reshape(LENGTH, HEADS, HEAD_DIM)
        values_all = qkv[:, 2 * D:].reshape(LENGTH, HEADS, HEAD_DIM)
        segs = LENGTH // SEG
        near, near_lse = lax.map(local_segment, (queries.reshape(segs, SEG, HEADS, HEAD_DIM), keys_all.reshape(segs, SEG, HEADS, HEAD_DIM), values_all.reshape(segs, SEG, HEADS, HEAD_DIM)))
        near_rows = near.reshape(far_rows, RATE, HEADS, HEAD_DIM)
        near_lse = near_lse.reshape(far_rows, RATE, HEADS)
        far, far_lse = lax.map(far_head, (jnp.moveaxis(pick(queries), 1, 0), jnp.moveaxis(pick(keys_all), 1, 0), jnp.moveaxis(pick(values_all), 1, 0)))
        far_t = jnp.moveaxis(far, 0, 1)
        far_lse_t = far_lse.T
        near_sel = near_rows[:, residue, head_ids]
        lse_sel = near_lse[:, residue, head_ids]
        top = jnp.maximum(lse_sel, far_lse_t)
        near_share = jnp.exp(lse_sel - top)
        far_share = jnp.exp(far_lse_t - top)
        mixed = (near_share[..., None] * near_sel + far_share[..., None] * far_t) / (near_share + far_share)[..., None]
        near_rows = near_rows.at[:, residue, head_ids].set(mixed)
        attn = near_rows.reshape(LENGTH, D).astype(jnp.bfloat16)
        projected = jnp.dot(attn, out_weight, preferred_element_type=jnp.float32)
        encoded = (inputs.astype(jnp.float32) + projected).astype(jnp.bfloat16)
        grad_term = jnp.dot(attn.T, slide_grad, preferred_element_type=jnp.float32)
        return (carry + grad_term, encoded)
    grad_total, encoded = lax.scan(one_slide, jnp.zeros((D, D), jnp.float32), (tile_rows, block_dest, cotangent))
    return (encoded, grad_total)
```

```python
import functools

import jax
import jax.numpy as jnp
from jax import lax
from jax.experimental import pallas as pl
from jax.experimental.pallas import tpu as pltpu
from jax.sharding import PartitionSpec as P

WIDTH = 768
HEADS = 12
HEAD_DIM = 64
BLK = 128
SEG = 512
RATE = 16
ROWS = 2048
SHARDS = 32
SLIDES = 4
SEGS = ROWS // SEG
STRIDE = 32
PAIRS = HEADS // 2
GROUPS = WIDTH // 128
FAR_OWNERS = 2 * HEADS
MESH = pl.DeviceIdType.MESH

score_scale = 0.125
norm_eps = 1e-06


def lanes(group):
    return slice(128 * group, 128 * group + 128)


def row_class(shard):
    return RATE * lax.rem(shard, 2) + lax.div(shard, 2)


def peer(me, step):
    z, x, c = lax.div(me, 8), lax.rem(lax.div(me, 2), 4), lax.rem(me, 2)
    dz = lax.rem(step, 4)
    dx = lax.rem(step + lax.div(step, 8), 4)
    dc = lax.rem(lax.div(step, 4), 2)
    return lax.rem(z + dz, 4) * 8 + lax.rem(x + dx, 4) * 2 + lax.rem(c + dc, 2)


def normalize(values, gain):
    center = values - jnp.mean(values, axis=-1, keepdims=True)
    spread = jnp.mean(center * center, axis=-1, keepdims=True)
    return (center * lax.rsqrt(spread + norm_eps) * gain).astype(jnp.bfloat16)


def dot(a, b):
    return jnp.dot(a, b, preferred_element_type=jnp.float32)


def dot_t(a, b):
    return lax.dot_general(a, b, (((1,), (1,)), ((), ())), preferred_element_type=jnp.float32)


def iota(shape, dim):
    return lax.broadcasted_iota(jnp.int32, shape, dim)


def one_hot(mask):
    return jnp.where(mask, 1.0, 0.0).astype(jnp.bfloat16)


def wait_bytes(ref, sem):
    pltpu.make_async_copy(ref, ref, sem).wait()


def target_rows(dest_rows):
    dests = dest_rows.astype(jnp.bfloat16)
    spread = one_hot(iota((128, ROWS), 0) == iota((128, ROWS), 1) % 64)
    wide = dot(dests, spread)
    of_source = iota((SHARDS, ROWS), 0) == iota((SHARDS, ROWS), 1) // 64
    dest = jnp.sum(jnp.where(of_source, wide, 0.0), axis=0, keepdims=True)
    dest_int = dest.astype(jnp.int32)
    named = jnp.where(iota((SHARDS, ROWS), 0) == dest_int, 1.0, 0.0)
    row = iota((ROWS, 128), 0)
    first = one_hot(jnp.logical_and(row // 64 == iota((ROWS, 128), 1), row % 4 == 0))
    has = dot(named.astype(jnp.bfloat16), first)
    earlier = one_hot(iota((128, 128), 0) < iota((128, 128), 1))
    rank = dot(has.astype(jnp.bfloat16), earlier)
    back = one_hot(iota((128, ROWS), 0) == iota((128, ROWS), 1) // 64)
    rank_wide = dot(rank.astype(jnp.bfloat16), back)
    slot = jnp.sum(named * rank_wide, axis=0, keepdims=True).astype(jnp.int32)
    within = iota((1, ROWS), 1) % 4
    return (slot // 4) * SEG + dest_int * 16 + (slot % 4) * 4 + within


def kernel(
    x_hbm, dest_ref, gain_ref, wqkv_hbm, wout_hbm, cot_hbm, enc_hbm, grad_ref,
    xb, xf, send1, recv1, dall, send2, recv2, place, kv, qf, qd, farsend, farrecv,
    wqkv, wfar, wout, normed, qkv, attn, lse, encst, gsend, grecv, ysend, yrecv, ysum, fin,
    bsem, ssem1, rsem1, dssem, drsem, ssem2, rsem2, kvs, kvr, fss, frs,
    gss, grs, yss, yrs, css, crs, xsem, wsem, osem, csem, esem,
):
    me = lax.axis_index("seq")
    dp = lax.axis_index("dp")
    core = lax.rem(me, 2)
    mate = me + 1 - 2 * core
    head = lax.div(me, 2)
    seg_base, attn_base, grad_base = 0, SEG, 2 * SEG

    load_x = pltpu.make_async_copy(x_hbm, xb, xsem)
    load_x.start()
    load_w = pltpu.make_async_copy(wqkv_hbm, wqkv, wsem)
    load_w.start()
    load_o = pltpu.make_async_copy(wout_hbm, wout, osem)
    load_o.start()

    barrier = pltpu.get_barrier_semaphore()

    def greet(step, _):
        pl.semaphore_signal(
            barrier, inc=1, device_id={"seq": peer(me, step)}, device_id_type=MESH
        )
        return 0

    lax.fori_loop(1, SHARDS, greet, 0)
    for step in range(1, SLIDES):
        pl.semaphore_signal(
            barrier, inc=1, device_id={"dp": lax.rem(dp + step, SLIDES)}, device_id_type=MESH
        )

    load_x.wait()

    def widen(index, _):
        rows = pl.ds(pl.multiple_of(index * 256, 256), 256)
        for group in range(GROUPS):
            xf[group, rows, :] = xb[rows, lanes(group)].astype(jnp.float32)
        return 0

    lax.fori_loop(0, ROWS // 256, widen, 0)
    load_c = pltpu.make_async_copy(cot_hbm, xb, csem)
    load_c.start()
    pl.semaphore_wait(barrier, SHARDS - 1 + SLIDES - 1)

    def tell(step, _):
        to = peer(me, step)
        pltpu.make_async_remote_copy(
            src_ref=dest_ref, dst_ref=dall.at[me], send_sem=dssem, recv_sem=drsem,
            device_id={"seq": to}, device_id_type=MESH,
        ).start()
        return 0

    lax.fori_loop(1, SHARDS, tell, 0)
    pltpu.make_async_copy(dest_ref, dall.at[me], drsem).start()

    def pack(to):
        rows = pl.ds(row_class(to), 64, stride=STRIDE)
        for group in range(GROUPS):
            send1[to, :, lanes(group)] = xf[group, rows, :].astype(jnp.bfloat16)

    def scatter(step, _):
        to = peer(me, step)
        pack(to)
        pltpu.make_async_remote_copy(
            src_ref=send1.at[to], dst_ref=recv1.at[me], send_sem=ssem1, recv_sem=rsem1,
            device_id={"seq": to}, device_id_type=MESH,
        ).start()
        return 0

    lax.fori_loop(1, SHARDS, scatter, 0)
    pack(me)
    pltpu.make_async_copy(send1.at[me], recv1.at[me], rsem1).start()

    wait_bytes(dall, drsem)
    target = target_rows(jnp.max(dall[...].astype(jnp.float32), axis=1))

    def build(part, _):
        rows = iota((SEG, ROWS), 0) + part * SEG
        place[part] = one_hot(rows == target)
        return 0

    lax.fori_loop(0, SEGS, build, 0)
    load_w.wait()
    pair_at = lax.div(head, 2) * 128
    for part in range(3):
        at = pl.multiple_of(jnp.minimum(pair_at, WIDTH - 128) + part * WIDTH, 128)
        wfar[:, part * 128 : (part + 1) * 128] = wqkv[:, pl.ds(at, 128)]

    wait_bytes(recv1, rsem1)
    gathered = recv1.reshape(ROWS, WIDTH)

    def regroup(part, _):
        moved = dot(place[part], gathered[...]).astype(jnp.bfloat16)
        send2[part] = moved.reshape(SHARDS, 16, WIDTH)

        def give(step, _):
            to = peer(me, step)
            pltpu.make_async_remote_copy(
                src_ref=send2.at[part, to], dst_ref=recv2.at[part, me],
                send_sem=ssem2.at[part], recv_sem=rsem2.at[part],
                device_id={"seq": to}, device_id_type=MESH,
            ).start()
            return 0

        lax.fori_loop(1, SHARDS, give, 0)
        pltpu.make_async_copy(send2.at[part, me], recv2.at[part, me], rsem2.at[part]).start()
        return 0

    lax.fori_loop(0, SEGS, regroup, 0)

    gain = gain_ref[...]

    @pl.when(head < HEADS)
    def _():
        half = lax.rem(head, 2)
        lane = iota((256, 128), 1)
        mine = lane // HEAD_DIM == half

        def project(index, _):
            rows = pl.ds(pl.multiple_of(index * 256, 256), 256)
            out = dot(normalize(gathered[rows, :].astype(jnp.float32), gain), wfar[...])
            qf[rows, :] = jnp.where(mine, out[:, :128].astype(jnp.bfloat16).astype(jnp.float32) * score_scale, 0.0).astype(jnp.bfloat16)
            kv[core, 0, rows, :] = out[:, 128:256].astype(jnp.bfloat16)
            kv[core, 1, rows, :] = jnp.where(mine, out[:, 256:], 1.0).astype(jnp.bfloat16)
            return 0

        lax.fori_loop(0, ROWS // 256, project, 0)
        swap = pltpu.make_async_remote_copy(
            src_ref=kv.at[core], dst_ref=kv.at[core], send_sem=kvs, recv_sem=kvr,
            device_id={"seq": mate}, device_id_type=MESH,
        )
        swap.start()

        def reorder(part, _):
            at = pl.ds(pl.multiple_of(part * SEG, SEG), SEG)
            qd[at, :] = dot(place[part], qf[...]).astype(jnp.bfloat16)
            return 0

        lax.fori_loop(0, SEGS, reorder, 0)
        swap.wait()
        far_flat = farsend.reshape(ROWS, 128)

        def far(index, _):
            rows = pl.ds(pl.multiple_of(index * 256, 256), 256)
            queries = qd[rows, :]
            scores = [dot_t(queries, kv[side, 0]) for side in range(2)]
            peak = jnp.maximum(
                jnp.max(scores[0], axis=-1, keepdims=True),
                jnp.max(scores[1], axis=-1, keepdims=True),
            )
            accum = jnp.zeros((256, 128), jnp.float32)
            for side in range(2):
                weights = jnp.exp(scores[side] - peak).astype(jnp.bfloat16)
                accum = accum + dot(weights, kv[side, 1])
            total = pltpu.roll(accum, 64, 1)
            mixed = accum / total
            level = peak + jnp.log(jnp.where(mine, 1.0, accum))
            high = level.astype(jnp.bfloat16).astype(jnp.float32)
            tail = jnp.where(lane % 64 < 32, high, level - high)
            far_flat[rows, :] = jnp.where(mine, mixed, tail).astype(jnp.bfloat16)
            return 0

        lax.fori_loop(0, ROWS // 256, far, 0)

        def give_far(step, _):
            to = peer(me, step)
            pltpu.make_async_remote_copy(
                src_ref=farsend.at[:, to], dst_ref=farrecv.at[me], send_sem=fss, recv_sem=frs,
                device_id={"seq": to}, device_id_type=MESH,
            ).start()
            return 0

        lax.fori_loop(1, SHARDS, give_far, 0)
        pltpu.make_async_copy(farsend.at[:, me], farrecv.at[me], frs).start()

    wait_bytes(farrecv, frs)
    load_c.wait()
    load_o.wait()
    low = iota((SEG, 128), 1) < HEAD_DIM
    low_far = iota((16, 128), 1) < HEAD_DIM

    def segment(part, _):
        wait_bytes(recv2.at[part], rsem2.at[part])
        for src in range(SHARDS):
            shift = RATE * (src % 2) + src // 2
            rows = pl.ds(seg_base + shift, 16, stride=STRIDE)
            for group in range(GROUPS):
                xf[group, rows, :] = recv2[part, src, :, lanes(group)].astype(jnp.float32)

        def norm_step(index, _):
            at = pl.multiple_of(index * 128, 128)
            normed[pl.ds(at, 128), :] = normalize(
                jnp.concatenate(
                    [xf[group, pl.ds(seg_base + at, 128), :] for group in range(GROUPS)], axis=1
                ),
                gain,
            )
            return 0

        lax.fori_loop(0, SEG // 128, norm_step, 0)

        def project(index, _):
            cols = pl.ds(pl.multiple_of(index * 384, 384), 384)
            qkv[:, cols] = dot(normed[...], wqkv[:, cols]).astype(jnp.bfloat16)
            return 0

        lax.fori_loop(0, 3 * WIDTH // 384, project, 0)

        def near(pair, _):
            at = pl.multiple_of(pair * 128, 128)
            queries = qkv[:, pl.ds(at, 128)].astype(jnp.float32) * score_scale
            keys = qkv[:, pl.ds(at + WIDTH, 128)]
            values = qkv[:, pl.ds(at + 2 * WIDTH, 128)].astype(jnp.float32)
            accums, peaks = [], []
            for side in range(2):
                mine = low if side == 0 else jnp.logical_not(low)
                scores = dot_t(jnp.where(mine, queries, 0.0).astype(jnp.bfloat16), keys)
                peak = jnp.max(scores, axis=-1, keepdims=True)
                weights = jnp.exp(scores - peak).astype(jnp.bfloat16)
                accums.append(dot(weights, jnp.where(mine, values, 1.0).astype(jnp.bfloat16)))
                peaks.append(peak)
            total = pltpu.roll(jnp.where(low, accums[1], accums[0]), 64, 1)
            xf[pair, pl.ds(attn_base, SEG), :] = jnp.where(low, accums[0], accums[1]) / total
            lse[pair] = jnp.where(low, peaks[0], peaks[1]) + jnp.log(total)
            return 0

        lax.fori_loop(0, PAIRS, near, 0)

        for src in range(FAR_OWNERS):
            number = src // 2
            pair, half = number // 2, number % 2
            shift = RATE * (src % 2) + number
            rows = pl.ds(attn_base + shift, 16, stride=STRIDE)
            near_part = xf[pair, rows, :]
            near_lse = lse[pair, pl.ds(shift, 16, stride=STRIDE), :]
            far_part = farrecv[src, part].astype(jnp.float32)
            other = HEAD_DIM * (1 - half)
            far_lse = far_part[:, other : other + 1] + far_part[:, other + 32 : other + 33]
            top = jnp.maximum(near_lse, far_lse)
            near_share = jnp.exp(near_lse - top)
            far_share = jnp.exp(far_lse - top)
            mixed = (near_share * near_part + far_share * far_part) / (near_share + far_share)
            mine = low_far if half == 0 else jnp.logical_not(low_far)
            xf[pair, rows, :] = jnp.where(mine, mixed, near_part)

        for group in range(GROUPS):
            attn[:, lanes(group)] = xf[group, pl.ds(attn_base, SEG), :].astype(jnp.bfloat16)
        seg_at = pl.multiple_of(part * SEG, SEG)

        def finish(index, _):
            cols = pl.ds(pl.multiple_of(index * 256, 256), 256)
            projected = dot(attn[...], wout[:, cols])
            for sub in range(2):
                part_in = xf[2 * index + sub, pl.ds(seg_base, SEG), :]
                at = pl.multiple_of(index * 256 + sub * 128, 128)
                encst[part, :, pl.ds(at, 128)] = (part_in + projected[:, lanes(sub)]).astype(
                    jnp.bfloat16
                )
            term = lax.dot_general(
                attn[...], xb[pl.ds(seg_at, SEG), cols], (((0,), (0,)), ((), ())),
                preferred_element_type=jnp.float32,
            )
            for sub in range(2):
                held = xf[2 * index + sub, pl.ds(grad_base, WIDTH), :]
                piece = term[:, lanes(sub)]
                xf[2 * index + sub, pl.ds(grad_base, WIDTH), :] = jnp.where(
                    part == 0, piece, held + piece
                )
            return 0

        lax.fori_loop(0, WIDTH // 256, finish, 0)
        pltpu.make_async_copy(
            encst.at[part], enc_hbm.at[pl.ds(seg_at, SEG)], esem.at[part]
        ).start()
        return 0

    lax.fori_loop(0, SEGS, segment, 0)

    for chip in range(SHARDS // 2):
        for side in range(2):
            for group in range(3):
                gsend[2 * chip + side, :, lanes(group)] = xf[
                    3 * side + group, pl.ds(grad_base + 48 * chip, 48), :
                ].astype(jnp.bfloat16)

    def give_grad(step, _):
        to = peer(me, step)
        pltpu.make_async_remote_copy(
            src_ref=gsend.at[to], dst_ref=grecv.at[me], send_sem=gss, recv_sem=grs,
            device_id={"seq": to}, device_id_type=MESH,
        ).start()
        return 0

    lax.fori_loop(1, SHARDS, give_grad, 0)
    pltpu.make_async_copy(gsend.at[me], grecv.at[me], grs).start()
    wait_bytes(grecv, grs)
    ysend[...] = jnp.sum(grecv[...].astype(jnp.float32), axis=0).astype(jnp.bfloat16)
    for step in range(1, SLIDES):
        pltpu.make_async_remote_copy(
            src_ref=ysend, dst_ref=yrecv.at[dp], send_sem=yss, recv_sem=yrs,
            device_id={"dp": lax.rem(dp + step, SLIDES)}, device_id_type=MESH,
        ).start()
    pltpu.make_async_copy(ysend, yrecv.at[dp], yrs).start()
    wait_bytes(yrecv, yrs)
    whole = jnp.sum(yrecv[...].astype(jnp.float32), axis=0)
    ysum[0] = whole[:24]
    ysum[1] = whole[24:]
    last = pltpu.make_async_remote_copy(
        src_ref=ysum.at[1 - core], dst_ref=fin.at[core], send_sem=css, recv_sem=crs,
        device_id={"seq": mate}, device_id_type=MESH,
    )
    last.start()
    fin[core] = ysum[core]
    last.wait()
    grad_ref[:, :384] = fin[0]
    grad_ref[:, 384:] = fin[1]

    wait_bytes(dall.at[pl.ds(0, SHARDS - 1)], dssem)
    wait_bytes(send1.at[pl.ds(0, SHARDS - 1)], ssem1)
    for part in range(SEGS):
        wait_bytes(send2.at[part, pl.ds(0, SHARDS - 1)], ssem2.at[part])
        wait_bytes(encst.at[part], esem.at[part])

    @pl.when(head < HEADS)
    def _():
        wait_bytes(farsend.at[:, pl.ds(0, SHARDS - 1)], fss)

    wait_bytes(gsend.at[pl.ds(0, SHARDS - 1)], gss)
    wait_bytes(yrecv.at[pl.ds(0, SLIDES - 1)], yss)


def body(tile_rows, block_dest, norm_gain, qkv_weight, out_weight, cotangent):
    dests = jnp.pad(jnp.repeat(block_dest, 4, axis=1), ((0, 0), (0, 64)))
    dests = jnp.broadcast_to(dests, (8, 128))
    bf16, f32 = jnp.bfloat16, jnp.float32
    dma = pltpu.SemaphoreType.DMA
    anywhere = pl.BlockSpec(memory_space=pl.ANY)
    vmem = pl.BlockSpec(memory_space=pltpu.VMEM)
    encoded, grad = pl.pallas_call(
        kernel,
        out_shape=(
            jax.ShapeDtypeStruct((ROWS, WIDTH), bf16),
            jax.ShapeDtypeStruct((24, WIDTH), f32),
        ),
        in_specs=[anywhere, vmem, vmem, anywhere, anywhere, anywhere],
        out_specs=(anywhere, vmem),
        scratch_shapes=[
            pltpu.VMEM((ROWS, WIDTH), bf16),
            pltpu.VMEM((GROUPS, ROWS, 128), f32),
            pltpu.VMEM((SHARDS, 64, WIDTH), bf16),
            pltpu.VMEM((SHARDS, 64, WIDTH), bf16),
            pltpu.VMEM((SHARDS, 8, 128), jnp.int32),
            pltpu.VMEM((SEGS, SHARDS, 16, WIDTH), bf16),
            pltpu.VMEM((SEGS, SHARDS, 16, WIDTH), bf16),
            pltpu.VMEM((SEGS, SEG, ROWS), bf16),
            pltpu.VMEM((2, 2, ROWS, 128), bf16),
            pltpu.VMEM((ROWS, 128), bf16),
            pltpu.VMEM((ROWS, 128), bf16),
            pltpu.VMEM((SEGS, SHARDS, 16, 128), bf16),
            pltpu.VMEM((FAR_OWNERS, SEGS, 16, 128), bf16),
            pltpu.VMEM((WIDTH, 3 * WIDTH), bf16),
            pltpu.VMEM((WIDTH, 384), bf16),
            pltpu.VMEM((WIDTH, WIDTH), bf16),
            pltpu.VMEM((SEG, WIDTH), bf16),
            pltpu.VMEM((SEG, 3 * WIDTH), bf16),
            pltpu.VMEM((SEG, WIDTH), bf16),
            pltpu.VMEM((PAIRS, SEG, 128), f32),
            pltpu.VMEM((SEGS, SEG, WIDTH), bf16),
            pltpu.VMEM((SHARDS, 48, 384), bf16),
            pltpu.VMEM((SHARDS, 48, 384), bf16),
            pltpu.VMEM((48, 384), bf16),
            pltpu.VMEM((SLIDES, 48, 384), bf16),
            pltpu.VMEM((2, 24, 384), f32),
            pltpu.VMEM((2, 24, 384), f32),
            dma, dma, dma, dma, dma, dma((SEGS,)), dma((SEGS,)), dma, dma, dma, dma,
            dma, dma, dma, dma, dma, dma, dma, dma, dma, dma, dma((SEGS,)),
        ],
        compiler_params=pltpu.CompilerParams(
            collective_id=0, has_side_effects=True, vmem_limit_bytes=62 * 1024 * 1024
        ),
        name="slide_layer",
    )(
        tile_rows.reshape(ROWS, WIDTH), dests, norm_gain.reshape(1, WIDTH),
        qkv_weight, out_weight, cotangent.reshape(ROWS, WIDTH),
    )
    return encoded.reshape(1, ROWS, WIDTH), grad


def solution(mesh):
    return jax.shard_map(
        body,
        mesh=mesh,
        in_specs=(P("dp", "seq", None), P("dp", "seq"), P(), P(), P(), P("dp", "seq", None)),
        out_specs=(P("dp", "seq", None), P("seq", None)),
        check_vma=False,
    )
```

```python
import functools

import jax
import jax.numpy as jnp
from jax import lax
from jax.experimental import pallas as pl
from jax.experimental.pallas import tpu as pltpu
from jax.sharding import PartitionSpec as P

WIDTH = 768
HEADS = 12
HEAD_DIM = 64
BLK = 128
SEG = 512
RATE = 16
ROWS = 2048
SHARDS = 32
SLIDES = 4
SEGS = ROWS // SEG
STRIDE = 32
PAIRS = HEADS // 2
GROUPS = WIDTH // 128
FAR_OWNERS = 2 * HEADS
MESH = pl.DeviceIdType.MESH

score_scale = 0.125
norm_eps = 1e-06


def lanes(group):
    return slice(128 * group, 128 * group + 128)


def row_class(shard):
    return RATE * lax.rem(shard, 2) + lax.div(shard, 2)


def peer(me, step):
    z, x, c = lax.div(me, 8), lax.rem(lax.div(me, 2), 4), lax.rem(me, 2)
    dz = lax.rem(step, 4)
    dx = lax.rem(step + lax.div(step, 8), 4)
    dc = lax.rem(lax.div(step, 4), 2)
    return lax.rem(z + dz, 4) * 8 + lax.rem(x + dx, 4) * 2 + lax.rem(c + dc, 2)


def origin(me, step):
    z, x, c = lax.div(me, 8), lax.rem(lax.div(me, 2), 4), lax.rem(me, 2)
    dz = lax.rem(step, 4)
    dx = lax.rem(step + lax.div(step, 8), 4)
    dc = lax.rem(lax.div(step, 4), 2)
    return lax.rem(z + 4 - dz, 4) * 8 + lax.rem(x + 4 - dx, 4) * 2 + lax.rem(c + 2 - dc, 2)


def normalize(values, gain):
    center = values - jnp.mean(values, axis=-1, keepdims=True)
    spread = jnp.mean(center * center, axis=-1, keepdims=True)
    return (center * lax.rsqrt(spread + norm_eps) * gain).astype(jnp.bfloat16)


def dot(a, b):
    return jnp.dot(a, b, preferred_element_type=jnp.float32)


def dot_t(a, b):
    return lax.dot_general(a, b, (((1,), (1,)), ((), ())), preferred_element_type=jnp.float32)


def iota(shape, dim):
    return lax.broadcasted_iota(jnp.int32, shape, dim)


def one_hot(mask):
    return jnp.where(mask, 1.0, 0.0).astype(jnp.bfloat16)


def wait_bytes(ref, sem):
    pltpu.make_async_copy(ref, ref, sem).wait()


def target_rows(me, dest_rows):
    dests = dest_rows.astype(jnp.bfloat16)
    spread = one_hot(iota((128, ROWS), 0) == iota((128, ROWS), 1) % 64)
    wide = dot(dests, spread)
    of_source = iota((SHARDS, ROWS), 0) == iota((SHARDS, ROWS), 1) // 64
    dest = jnp.sum(jnp.where(of_source, wide, 0.0), axis=0, keepdims=True)
    dest_int = dest.astype(jnp.int32)
    named = jnp.where(iota((SHARDS, ROWS), 0) == dest_int, 1.0, 0.0)
    row = iota((ROWS, 128), 0)
    first = one_hot(jnp.logical_and(row // 64 == iota((ROWS, 128), 1), row % 4 == 0))
    has = dot(named.astype(jnp.bfloat16), first)
    earlier = one_hot(origin(me, iota((128, 128), 0)) < origin(me, iota((128, 128), 1)))
    rank = dot(has.astype(jnp.bfloat16), earlier)
    back = one_hot(iota((128, ROWS), 0) == iota((128, ROWS), 1) // 64)
    rank_wide = dot(rank.astype(jnp.bfloat16), back)
    slot = jnp.sum(named * rank_wide, axis=0, keepdims=True).astype(jnp.int32)
    within = iota((1, ROWS), 1) % 4
    return (slot // 4) * SEG + dest_int * 16 + (slot % 4) * 4 + within


def kernel(
    x_hbm, dest_ref, gain_ref, wqkv_hbm, wout_hbm, cot_hbm, enc_hbm, grad_ref,
    xb, xf, send1, recv1, dall, send2, recv2, place, kv, qf, qd, farsend, farrecv,
    wqkv, wfar, wout, normed, qkv, attn, lse, encst, gsend, gmate, gpart, grecv, ysend, yrecv, ysum, fin,
    ssem1, rsem1, dssem, drsem, ssem2, rsem2, kvs, kvr, fss, frs,
    jss, jrs, gss, grs, yss, yrs, css, crs, xsem, wsem, osem, csem, esem,
):
    me = lax.axis_index("seq")
    dp = lax.axis_index("dp")
    core = lax.rem(me, 2)
    mate = me + 1 - 2 * core
    head = lax.div(me, 2)
    seg_base, attn_base, grad_base = 0, SEG, 2 * SEG

    load_x = pltpu.make_async_copy(x_hbm, xb, xsem)
    load_x.start()
    load_w = pltpu.make_async_copy(wqkv_hbm, wqkv, wsem)
    load_w.start()
    load_o = pltpu.make_async_copy(wout_hbm, wout, osem)
    load_o.start()

    barrier = pltpu.get_barrier_semaphore()

    def greet(step, _):
        pl.semaphore_signal(
            barrier, inc=1, device_id={"seq": peer(me, step)}, device_id_type=MESH
        )
        return 0

    lax.fori_loop(1, SHARDS, greet, 0)
    for step in range(1, SLIDES):
        pl.semaphore_signal(
            barrier, inc=1, device_id={"dp": lax.rem(dp + step, SLIDES)}, device_id_type=MESH
        )

    load_x.wait()

    def widen(index, _):
        rows = pl.ds(pl.multiple_of(index * 256, 256), 256)
        for group in range(GROUPS):
            xf[group, rows, :] = xb[rows, lanes(group)].astype(jnp.float32)
        return 0

    lax.fori_loop(0, ROWS // 256, widen, 0)
    load_c = pltpu.make_async_copy(cot_hbm, xb, csem)
    load_c.start()
    pl.semaphore_wait(barrier, SHARDS - 1 + SLIDES - 1)

    def tell(step, _):
        to = peer(me, step)
        pltpu.make_async_remote_copy(
            src_ref=dest_ref, dst_ref=dall.at[step], send_sem=dssem, recv_sem=drsem,
            device_id={"seq": to}, device_id_type=MESH,
        ).start()
        return 0

    lax.fori_loop(1, SHARDS, tell, 0)
    pltpu.make_async_copy(dest_ref, dall.at[0], drsem).start()

    def pack(to):
        rows = pl.ds(row_class(to), 64, stride=STRIDE)
        for group in range(GROUPS):
            send1[to, :, lanes(group)] = xf[group, rows, :].astype(jnp.bfloat16)

    def scatter(step, _):
        to = peer(me, step)
        pack(to)
        pltpu.make_async_remote_copy(
            src_ref=send1.at[to], dst_ref=recv1.at[step], send_sem=ssem1,
            recv_sem=rsem1.at[lax.div(step, 8)],
            device_id={"seq": to}, device_id_type=MESH,
        ).start()
        return 0

    lax.fori_loop(1, SHARDS, scatter, 0)
    pack(me)
    pltpu.make_async_copy(send1.at[me], recv1.at[0], rsem1.at[0]).start()

    wait_bytes(dall, drsem)
    target = target_rows(me, jnp.max(dall[...].astype(jnp.float32), axis=1))

    def build(part, _):
        rows = iota((SEG, ROWS), 0) + part * SEG
        place[part] = one_hot(rows == target)
        return 0

    lax.fori_loop(0, SEGS, build, 0)
    load_w.wait()
    pair_at = lax.div(head, 2) * 128
    for part in range(3):
        at = pl.multiple_of(jnp.minimum(pair_at, WIDTH - 128) + part * WIDTH, 128)
        wfar[:, part * 128 : (part + 1) * 128] = wqkv[:, pl.ds(at, 128)]

    gathered = recv1.reshape(ROWS, WIDTH)
    gain = gain_ref[...]
    half = lax.rem(head, 2)

    def far_project(group):
        mine = iota((SEG, 128), 1) // HEAD_DIM == half
        rows = slice(group * SEG, group * SEG + SEG)
        out = dot(normalize(gathered[rows, :].astype(jnp.float32), gain), wfar[...])
        out = out.astype(jnp.bfloat16)
        zero, one = jnp.bfloat16(0.0), jnp.bfloat16(1.0)
        qf[rows, :] = jnp.where(mine, out[:, :128] * jnp.bfloat16(score_scale), zero)
        kv[core, 0, rows, :] = out[:, 128:256]
        kv[core, 1, rows, :] = jnp.where(mine, out[:, 256:], one)

    def moved(part, group):
        rows = slice(group * SEG, group * SEG + SEG)
        return dot(place[part, :, rows], gathered[rows, :])

    for group in range(SEGS - 1):
        wait_bytes(recv1.at[pl.ds(8 * group, 8)], rsem1.at[group])

        def regroup(part, _, group=group):
            term = moved(part, group)
            at = pl.ds(pl.multiple_of(part * SEG, SEG), SEG)
            for cols in range(GROUPS):
                piece = term[:, lanes(cols)]
                xf[cols, at, :] = piece if group == 0 else xf[cols, at, :] + piece
            return 0

        lax.fori_loop(0, SEGS, regroup, 0)
        pl.when(head < HEADS)(functools.partial(far_project, group))

    def deliver(part, _):
        term = moved(part, SEGS - 1)
        at = pl.ds(pl.multiple_of(part * SEG, SEG), SEG)
        for cols in range(GROUPS):
            piece = (xf[cols, at, :] + term[:, lanes(cols)]).astype(jnp.bfloat16)
            send2[part, :, :, lanes(cols)] = piece.reshape(SHARDS, 16, 128)

        def give(step, _):
            to = peer(me, step)
            pltpu.make_async_remote_copy(
                src_ref=send2.at[part, to], dst_ref=recv2.at[part, me],
                send_sem=ssem2.at[part], recv_sem=rsem2.at[part],
                device_id={"seq": to}, device_id_type=MESH,
            ).start()
            return 0

        lax.fori_loop(1, SHARDS, give, 0)
        pltpu.make_async_copy(send2.at[part, me], recv2.at[part, me], rsem2.at[part]).start()
        return 0

    wait_bytes(recv1.at[pl.ds(24, 8)], rsem1.at[SEGS - 1])
    lax.fori_loop(0, 2, deliver, 0)

    @pl.when(head < HEADS)
    def _():
        far_project(SEGS - 1)
        swap = pltpu.make_async_remote_copy(
            src_ref=kv.at[core], dst_ref=kv.at[core], send_sem=kvs, recv_sem=kvr,
            device_id={"seq": mate}, device_id_type=MESH,
        )
        swap.start()

        def reorder(part, _):
            at = pl.ds(pl.multiple_of(part * SEG, SEG), SEG)
            qd[at, :] = dot(place[part], qf[...]).astype(jnp.bfloat16)
            return 0

        lax.fori_loop(0, SEGS, reorder, 0)
        swap.wait()
        far_flat = farsend.reshape(ROWS, 128)
        lane = iota((SEG, 128), 1)
        mine = lane // HEAD_DIM == half

        def far(index, _):
            rows = pl.ds(pl.multiple_of(index * SEG, SEG), SEG)
            queries = qd[rows, :]
            blocks = [(side, slice(at, at + SEG)) for side in range(2) for at in range(0, ROWS, SEG)]
            upcoming = dot_t(queries, kv[0, 0, blocks[0][1], :])
            peak = accum = None
            for number, (side, keys) in enumerate(blocks):
                scores = upcoming
                if number + 1 < len(blocks):
                    after, cut = blocks[number + 1]
                    upcoming = dot_t(queries, kv[after, 0, cut, :])
                top = jnp.max(scores, axis=-1, keepdims=True)
                if number:
                    top = jnp.maximum(peak, top)
                    accum = accum * jnp.exp(peak - top)
                term = dot(jnp.exp(scores - top).astype(jnp.bfloat16), kv[side, 1, keys, :])
                accum = accum + term if number else term
                peak = top
            total = pltpu.roll(accum, 64, 1)
            mixed = accum / total
            level = peak + jnp.log(jnp.where(mine, 1.0, accum))
            high = level.astype(jnp.bfloat16).astype(jnp.float32)
            tail = jnp.where(lane % 64 < 32, high, level - high)
            far_flat[rows, :] = jnp.where(mine, mixed, tail).astype(jnp.bfloat16)
            return 0

        lax.fori_loop(0, SEGS, far, 0)

        def give_far(step, _):
            to = peer(me, step)
            pltpu.make_async_remote_copy(
                src_ref=farsend.at[:, to], dst_ref=farrecv.at[me], send_sem=fss, recv_sem=frs,
                device_id={"seq": to}, device_id_type=MESH,
            ).start()
            return 0

        lax.fori_loop(1, SHARDS, give_far, 0)
        pltpu.make_async_copy(farsend.at[:, me], farrecv.at[me], frs).start()

    lax.fori_loop(2, SEGS, deliver, 0)
    wait_bytes(farrecv, frs)
    load_c.wait()
    load_o.wait()
    low = iota((SEG, 128), 1) < HEAD_DIM
    low_far = iota((16, 128), 1) < HEAD_DIM

    def segment(part, _):
        wait_bytes(recv2.at[part], rsem2.at[part])
        for src in range(SHARDS):
            shift = RATE * (src % 2) + src // 2
            rows = pl.ds(seg_base + shift, 16, stride=STRIDE)
            for group in range(GROUPS):
                xf[group, rows, :] = recv2[part, src, :, lanes(group)].astype(jnp.float32)

        for at in range(0, SEG, 128):
            normed[at : at + 128, :] = normalize(
                jnp.concatenate(
                    [xf[group, pl.ds(seg_base + at, 128), :] for group in range(GROUPS)], axis=1
                ),
                gain,
            )

        def project(index):
            for kind in range(3):
                cols = slice(kind * WIDTH + index * 256, kind * WIDTH + index * 256 + 256)
                qkv[:, cols] = dot(normed[...], wqkv[:, cols]).astype(jnp.bfloat16)

        def operands(number):
            pair, side = number // 2, number % 2
            mine = low if side == 0 else jnp.logical_not(low)
            queries = qkv[:, lanes(pair)] * jnp.bfloat16(score_scale)
            values = qkv[:, lanes(pair + 2 * PAIRS)]
            return (
                jnp.where(mine, queries, jnp.zeros_like(queries)),
                qkv[:, lanes(pair + PAIRS)],
                jnp.where(mine, values, jnp.ones_like(values)),
            )

        def start_head(number):
            queries, keys, values = operands(number)
            return dot_t(queries, keys), values

        project(0)
        upcoming = start_head(0)
        kept = []
        for number in range(HEADS):
            scores, values = upcoming
            if number % 4 == 0 and number + 4 < HEADS:
                project(number // 4 + 1)
            if number + 1 < HEADS:
                upcoming = start_head(number + 1)
            peak = jnp.max(scores, axis=-1, keepdims=True)
            weights = jnp.exp(scores - peak).astype(jnp.bfloat16)
            kept.append((dot(weights, values), peak))
            if number % 2:
                (accum0, peak0), (accum1, peak1) = kept
                kept = []
                total = pltpu.roll(jnp.where(low, accum1, accum0), 64, 1)
                pair = number // 2
                xf[pair, pl.ds(attn_base, SEG), :] = jnp.where(low, accum0, accum1) / total
                lse[pair] = jnp.where(low, peak0, peak1) + jnp.log(total)

        for src in range(FAR_OWNERS):
            number = src // 2
            pair, half = number // 2, number % 2
            shift = RATE * (src % 2) + number
            rows = pl.ds(attn_base + shift, 16, stride=STRIDE)
            near_part = xf[pair, rows, :]
            near_lse = lse[pair, pl.ds(shift, 16, stride=STRIDE), :]
            far_part = farrecv[src, part].astype(jnp.float32)
            other = HEAD_DIM * (1 - half)
            far_lse = far_part[:, other : other + 1] + far_part[:, other + 32 : other + 33]
            top = jnp.maximum(near_lse, far_lse)
            near_share = jnp.exp(near_lse - top)
            far_share = jnp.exp(far_lse - top)
            mixed = (near_share * near_part + far_share * far_part) / (near_share + far_share)
            mine = low_far if half == 0 else jnp.logical_not(low_far)
            xf[pair, rows, :] = jnp.where(mine, mixed, near_part)

        for group in range(GROUPS):
            attn[:, lanes(group)] = xf[group, pl.ds(attn_base, SEG), :].astype(jnp.bfloat16)
        seg_at = pl.multiple_of(part * SEG, SEG)

        for index in range(3):
            cols = slice(index * 256, index * 256 + 256)
            projected = dot(attn[...], wout[:, cols])
            term = lax.dot_general(
                attn[...], xb[pl.ds(seg_at, SEG), cols], (((0,), (0,)), ((), ())),
                preferred_element_type=jnp.float32,
            )
            for sub in range(2):
                group = 2 * index + sub
                encst[part, :, lanes(group)] = (
                    xf[group, pl.ds(seg_base, SEG), :] + projected[:, lanes(sub)]
                ).astype(jnp.bfloat16)
                held = xf[group, pl.ds(grad_base, WIDTH), :]
                piece = term[:, lanes(sub)]
                xf[group, pl.ds(grad_base, WIDTH), :] = jnp.where(part == 0, piece, held + piece)

        pltpu.make_async_copy(
            encst.at[part], enc_hbm.at[pl.ds(seg_at, SEG)], esem.at[part]
        ).start()
        return 0

    lax.fori_loop(0, SEGS, segment, 0)

    for side in range(2):
        for group in range(3):
            gsend[side, :, lanes(group)] = xf[
                3 * side + group, pl.ds(grad_base, WIDTH), :
            ].astype(jnp.bfloat16)
    join = pltpu.make_async_remote_copy(
        src_ref=gsend.at[1 - core], dst_ref=gmate, send_sem=jss, recv_sem=jrs,
        device_id={"seq": mate}, device_id_type=MESH,
    )
    join.start()
    join.wait()
    both = gsend[core].astype(jnp.float32) + gmate[...].astype(jnp.float32)
    gpart[...] = both.astype(jnp.bfloat16).reshape(SHARDS // 2, 48, 384)

    def give_grad(step, _):
        to = lax.rem(lax.div(me, 8) + lax.rem(step, 4), 4) * 8 + lax.rem(
            lax.rem(lax.div(me, 2), 4) + lax.rem(step + lax.div(step, 4), 4), 4
        ) * 2 + core
        pltpu.make_async_remote_copy(
            src_ref=gpart.at[lax.div(to, 2)], dst_ref=grecv.at[head], send_sem=gss, recv_sem=grs,
            device_id={"seq": to}, device_id_type=MESH,
        ).start()
        return 0

    lax.fori_loop(1, SHARDS // 2, give_grad, 0)
    pltpu.make_async_copy(gpart.at[head], grecv.at[head], grs).start()
    wait_bytes(grecv, grs)
    ysend[...] = jnp.sum(grecv[...].astype(jnp.float32), axis=0).astype(jnp.bfloat16)
    for step in range(1, SLIDES):
        pltpu.make_async_remote_copy(
            src_ref=ysend, dst_ref=yrecv.at[dp], send_sem=yss, recv_sem=yrs,
            device_id={"dp": lax.rem(dp + step, SLIDES)}, device_id_type=MESH,
        ).start()
    pltpu.make_async_copy(ysend, yrecv.at[dp], yrs).start()
    wait_bytes(yrecv, yrs)
    whole = jnp.sum(yrecv[...].astype(jnp.float32), axis=0)
    ysum[0] = whole[:24]
    ysum[1] = whole[24:]
    last = pltpu.make_async_remote_copy(
        src_ref=ysum.at[1 - core], dst_ref=fin.at[core], send_sem=css, recv_sem=crs,
        device_id={"seq": mate}, device_id_type=MESH,
    )
    last.start()
    fin[core] = ysum[core]
    last.wait()
    grad_ref[:, :384] = fin[0]
    grad_ref[:, 384:] = fin[1]

    wait_bytes(dall.at[pl.ds(0, SHARDS - 1)], dssem)
    wait_bytes(send1.at[pl.ds(0, SHARDS - 1)], ssem1)
    for part in range(SEGS):
        wait_bytes(send2.at[part, pl.ds(0, SHARDS - 1)], ssem2.at[part])
        wait_bytes(encst.at[part], esem.at[part])

    @pl.when(head < HEADS)
    def _():
        wait_bytes(farsend.at[:, pl.ds(0, SHARDS - 1)], fss)

    wait_bytes(gpart.at[pl.ds(0, SHARDS // 2 - 1)], gss)
    wait_bytes(yrecv.at[pl.ds(0, SLIDES - 1)], yss)


def body(tile_rows, block_dest, norm_gain, qkv_weight, out_weight, cotangent):
    dests = jnp.pad(jnp.repeat(block_dest, 4, axis=1), ((0, 0), (0, 64)))
    dests = jnp.broadcast_to(dests, (8, 128))
    bf16, f32 = jnp.bfloat16, jnp.float32
    dma = pltpu.SemaphoreType.DMA
    anywhere = pl.BlockSpec(memory_space=pl.ANY)
    vmem = pl.BlockSpec(memory_space=pltpu.VMEM)
    encoded, grad = pl.pallas_call(
        kernel,
        out_shape=(
            jax.ShapeDtypeStruct((ROWS, WIDTH), bf16),
            jax.ShapeDtypeStruct((24, WIDTH), f32),
        ),
        in_specs=[anywhere, vmem, vmem, anywhere, anywhere, anywhere],
        out_specs=(anywhere, vmem),
        scratch_shapes=[
            pltpu.VMEM((ROWS, WIDTH), bf16),
            pltpu.VMEM((GROUPS, ROWS, 128), f32),
            pltpu.VMEM((SHARDS, 64, WIDTH), bf16),
            pltpu.VMEM((SHARDS, 64, WIDTH), bf16),
            pltpu.VMEM((SHARDS, 8, 128), jnp.int32),
            pltpu.VMEM((SEGS, SHARDS, 16, WIDTH), bf16),
            pltpu.VMEM((SEGS, SHARDS, 16, WIDTH), bf16),
            pltpu.VMEM((SEGS, SEG, ROWS), bf16),
            pltpu.VMEM((2, 2, ROWS, 128), bf16),
            pltpu.VMEM((ROWS, 128), bf16),
            pltpu.VMEM((ROWS, 128), bf16),
            pltpu.VMEM((SEGS, SHARDS, 16, 128), bf16),
            pltpu.VMEM((FAR_OWNERS, SEGS, 16, 128), bf16),
            pltpu.VMEM((WIDTH, 3 * WIDTH), bf16),
            pltpu.VMEM((WIDTH, 384), bf16),
            pltpu.VMEM((WIDTH, WIDTH), bf16),
            pltpu.VMEM((SEG, WIDTH), bf16),
            pltpu.VMEM((SEG, 3 * WIDTH), bf16),
            pltpu.VMEM((SEG, WIDTH), bf16),
            pltpu.VMEM((PAIRS, SEG, 128), f32),
            pltpu.VMEM((SEGS, SEG, WIDTH), bf16),
            pltpu.VMEM((2, WIDTH, 384), bf16),
            pltpu.VMEM((WIDTH, 384), bf16),
            pltpu.VMEM((SHARDS // 2, 48, 384), bf16),
            pltpu.VMEM((SHARDS // 2, 48, 384), bf16),
            pltpu.VMEM((48, 384), bf16),
            pltpu.VMEM((SLIDES, 48, 384), bf16),
            pltpu.VMEM((2, 24, 384), f32),
            pltpu.VMEM((2, 24, 384), f32),
            dma, dma((SEGS,)), dma, dma, dma((SEGS,)), dma((SEGS,)), dma, dma, dma, dma, dma, dma,
            dma, dma, dma, dma, dma, dma, dma, dma, dma, dma, dma((SEGS,)),
        ],
        compiler_params=pltpu.CompilerParams(
            collective_id=0, has_side_effects=True, vmem_limit_bytes=62 * 1024 * 1024
        ),
        name="slide_layer",
    )(
        tile_rows.reshape(ROWS, WIDTH), dests, norm_gain.reshape(1, WIDTH),
        qkv_weight, out_weight, cotangent.reshape(ROWS, WIDTH),
    )
    return encoded.reshape(1, ROWS, WIDTH), grad


def solution(mesh):
    return jax.shard_map(
        body,
        mesh=mesh,
        in_specs=(P("dp", "seq", None), P("dp", "seq"), P(), P(), P(), P("dp", "seq", None)),
        out_specs=(P("dp", "seq", None), P("seq", None)),
        check_vma=False,
    )
```

```python
import functools

import jax
import jax.numpy as jnp
from jax import lax
from jax.experimental import pallas as pl
from jax.experimental.pallas import tpu as pltpu
from jax.sharding import PartitionSpec as P

WIDTH = 768
HEADS = 12
HEAD_DIM = 64
BLK = 128
SEG = 512
RATE = 16
ROWS = 2048
SHARDS = 32
SLIDES = 4
SEGS = ROWS // SEG
STRIDE = 32
PAIRS = HEADS // 2
GROUPS = WIDTH // 128
FAR_OWNERS = 2 * HEADS
MESH = pl.DeviceIdType.MESH

score_scale = 0.125
norm_eps = 1e-06


def lanes(group):
    return slice(128 * group, 128 * group + 128)


def row_class(shard):
    return RATE * lax.rem(shard, 2) + lax.div(shard, 2)


def peer(me, step):
    z, x, c = lax.div(me, 8), lax.rem(lax.div(me, 2), 4), lax.rem(me, 2)
    dz = lax.rem(step, 4)
    dx = lax.rem(step + lax.div(step, 8), 4)
    dc = lax.rem(lax.div(step, 4), 2)
    return lax.rem(z + dz, 4) * 8 + lax.rem(x + dx, 4) * 2 + lax.rem(c + dc, 2)


def origin(me, step):
    z, x, c = lax.div(me, 8), lax.rem(lax.div(me, 2), 4), lax.rem(me, 2)
    dz = lax.rem(step, 4)
    dx = lax.rem(step + lax.div(step, 8), 4)
    dc = lax.rem(lax.div(step, 4), 2)
    return lax.rem(z + 4 - dz, 4) * 8 + lax.rem(x + 4 - dx, 4) * 2 + lax.rem(c + 2 - dc, 2)


def normalize(values, gain):
    center = values - jnp.mean(values, axis=-1, keepdims=True)
    spread = jnp.mean(center * center, axis=-1, keepdims=True)
    return (center * lax.rsqrt(spread + norm_eps) * gain).astype(jnp.bfloat16)


def dot(a, b):
    return jnp.dot(a, b, preferred_element_type=jnp.float32)


def dot_t(a, b):
    return lax.dot_general(a, b, (((1,), (1,)), ((), ())), preferred_element_type=jnp.float32)


def iota(shape, dim):
    return lax.broadcasted_iota(jnp.int32, shape, dim)


def one_hot(mask):
    return jnp.where(mask, 1.0, 0.0).astype(jnp.bfloat16)


def wait_bytes(ref, sem):
    pltpu.make_async_copy(ref, ref, sem).wait()


def target_rows(me, dest_rows):
    dests = dest_rows.astype(jnp.bfloat16)
    spread = one_hot(iota((128, ROWS), 0) == iota((128, ROWS), 1) % 64)
    wide = dot(dests, spread)
    of_source = iota((SHARDS, ROWS), 0) == iota((SHARDS, ROWS), 1) // 64
    dest = jnp.sum(jnp.where(of_source, wide, 0.0), axis=0, keepdims=True)
    dest_int = dest.astype(jnp.int32)
    named = jnp.where(iota((SHARDS, ROWS), 0) == dest_int, 1.0, 0.0)
    row = iota((ROWS, 128), 0)
    first = one_hot(jnp.logical_and(row // 64 == iota((ROWS, 128), 1), row % 4 == 0))
    has = dot(named.astype(jnp.bfloat16), first)
    earlier = one_hot(origin(me, iota((128, 128), 0)) < origin(me, iota((128, 128), 1)))
    rank = dot(has.astype(jnp.bfloat16), earlier)
    back = one_hot(iota((128, ROWS), 0) == iota((128, ROWS), 1) // 64)
    rank_wide = dot(rank.astype(jnp.bfloat16), back)
    slot = jnp.sum(named * rank_wide, axis=0, keepdims=True).astype(jnp.int32)
    within = iota((1, ROWS), 1) % 4
    return (slot // 4) * SEG + dest_int * 16 + (slot % 4) * 4 + within


def kernel(
    x_hbm, dest_ref, gain_ref, wqkv_hbm, wout_hbm, cot_hbm, enc_hbm, grad_ref,
    xb, xf, send1, recv1, dsend, dall, send2, recv2, place, ordered, classed, kv, qf, fout, farsend, farrecv,
    wqkv, wfar, wout, normed, qkv, mix, lse, grad, gsend, gmate, gpart, grecv, ysend, yrecv, ysum, fin,
    ssem1, rsem1, dssem, drsem, ssem2, rsem2, kvs, kvr, fss, frs,
    jss, jrs, gss, grs, yss, yrs, css, crs, xsem, wsem, osem, csem, esem,
):
    me = lax.axis_index("seq")
    dp = lax.axis_index("dp")
    core = lax.rem(me, 2)
    mate = me + 1 - 2 * core
    head = lax.div(me, 2)

    load_x = [
        pltpu.make_async_copy(
            x_hbm.at[pl.ds(at, SEG)], xb.at[pl.ds(at, SEG)], xsem.at[at // SEG]
        )
        for at in range(0, ROWS, SEG)
    ]
    for load in load_x:
        load.start()
    load_w = pltpu.make_async_copy(wqkv_hbm, wqkv, wsem)
    load_w.start()
    load_o = pltpu.make_async_copy(wout_hbm, wout, osem)
    load_o.start()

    barrier = pltpu.get_barrier_semaphore()

    def greet(step, _):
        pl.semaphore_signal(
            barrier, inc=1, device_id={"seq": peer(me, step)}, device_id_type=MESH
        )
        return 0

    lax.fori_loop(1, SHARDS, greet, 0)
    for step in range(1, SLIDES):
        pl.semaphore_signal(
            barrier, inc=1, device_id={"dp": lax.rem(dp + step, SLIDES)}, device_id_type=MESH
        )

    spread = one_hot(iota((16, 128), 0) == iota((16, 128), 1) // 4)
    dests = dot(dest_ref[...].astype(jnp.float32).astype(jnp.bfloat16), spread)
    dsend[...] = jnp.broadcast_to(dests, (8, 128)).astype(jnp.int32)

    def widen(index, _):
        wait_bytes(xb.at[pl.ds(0, SEG)], xsem.at[index])
        rows = pl.ds(pl.multiple_of(index * SEG, SEG), SEG)
        for group in range(GROUPS):
            xf[group, rows, :] = xb[rows, lanes(group)].astype(jnp.float32)
        return 0

    lax.fori_loop(0, SEGS, widen, 0)
    load_c = pltpu.make_async_copy(cot_hbm, xb, csem)
    load_c.start()
    pl.semaphore_wait(barrier, SHARDS - 1 + SLIDES - 1)

    def tell(step, _):
        to = peer(me, step)
        pltpu.make_async_remote_copy(
            src_ref=dsend, dst_ref=dall.at[step], send_sem=dssem, recv_sem=drsem,
            device_id={"seq": to}, device_id_type=MESH,
        ).start()
        return 0

    lax.fori_loop(1, SHARDS, tell, 0)
    pltpu.make_async_copy(dsend, dall.at[0], drsem).start()

    def pack(to):
        rows = pl.ds(row_class(to), 64, stride=STRIDE)
        for group in range(GROUPS):
            send1[to, :, lanes(group)] = xf[group, rows, :].astype(jnp.bfloat16)

    def scatter(step, _):
        to = peer(me, step)
        pack(to)
        pltpu.make_async_remote_copy(
            src_ref=send1.at[to], dst_ref=recv1.at[step], send_sem=ssem1,
            recv_sem=rsem1.at[lax.div(step, 8)],
            device_id={"seq": to}, device_id_type=MESH,
        ).start()
        return 0

    lax.fori_loop(1, SHARDS, scatter, 0)
    pack(me)
    pltpu.make_async_copy(send1.at[me], recv1.at[0], rsem1.at[0]).start()

    wait_bytes(dall, drsem)
    target = target_rows(me, jnp.max(dall[...].astype(jnp.float32), axis=1))

    def build(part, _):
        rows = iota((SEG, ROWS), 0) + part * SEG
        place[part] = one_hot(rows == target)
        return 0

    lax.fori_loop(0, SEGS, build, 0)
    row, col = iota((SEG, SEG), 0), iota((SEG, SEG), 1)
    ordered[...] = one_hot(col == 32 * (row % RATE) + 16 * (row % STRIDE // RATE) + row // STRIDE)
    classed[...] = one_hot(col == STRIDE * (row % 16) + row_class(row // 16))
    load_c.wait()

    def class_order(part, _):
        rows = pl.ds(pl.multiple_of(part * SEG, SEG), SEG)
        xb[rows, :] = dot(classed[...], xb[rows, :]).astype(jnp.bfloat16)
        return 0

    lax.fori_loop(0, SEGS, class_order, 0)
    load_w.wait()
    pair_at = lax.div(head, 2) * 128
    for part in range(3):
        at = pl.multiple_of(jnp.minimum(pair_at, WIDTH - 128) + part * WIDTH, 128)
        wfar[:, part * 128 : (part + 1) * 128] = wqkv[:, pl.ds(at, 128)]

    gathered = recv1.reshape(ROWS, WIDTH)
    gain = gain_ref[...].reshape(1, WIDTH)
    half = lax.rem(head, 2)

    def far_project(group):
        mine = iota((SEG, 128), 1) // HEAD_DIM == half
        rows = slice(group * SEG, group * SEG + SEG)
        out = dot(normalize(gathered[rows, :].astype(jnp.float32), gain), wfar[...])
        out = out.astype(jnp.bfloat16)
        zero, one = jnp.bfloat16(0.0), jnp.bfloat16(1.0)
        qf[rows, :] = jnp.where(mine, out[:, :128] * jnp.bfloat16(score_scale), zero)
        kv[core, 0, rows, :] = out[:, 128:256]
        kv[core, 1, rows, :] = jnp.where(mine, out[:, 256:], one)

    def swap(stage):
        rows = pl.ds(stage * 3 * SEG, 3 * SEG if stage == 0 else SEG)
        return pltpu.make_async_remote_copy(
            src_ref=kv.at[core, :, rows], dst_ref=kv.at[core, :, rows],
            send_sem=kvs.at[stage], recv_sem=kvr.at[stage],
            device_id={"seq": mate}, device_id_type=MESH,
        )

    blocks = [(side, slice(at, at + SEG)) for side in range(2) for at in range(0, ROWS, SEG)]

    def far_blocks(queries):
        accum = peak = None
        upcoming = dot_t(queries, kv[blocks[0][0], 0, blocks[0][1], :])
        for number, (side, keys) in enumerate(blocks):
            scores = upcoming
            if number + 1 < len(blocks):
                after, cut = blocks[number + 1]
                upcoming = dot_t(queries, kv[after, 0, cut, :])
            top = jnp.max(scores, axis=-1, keepdims=True)
            if peak is not None:
                top = jnp.maximum(peak, top)
                accum = accum * jnp.exp(peak - top)
            term = dot(jnp.exp(scores - top).astype(jnp.bfloat16), kv[side, 1, keys, :])
            accum = term if accum is None else accum + term
            peak = top
        return accum, peak

    def far_result(accum, peak):
        lane = iota((SEG, 128), 1)
        mine = lane // HEAD_DIM == half
        mixed = accum / pltpu.roll(accum, 64, 1)
        level = peak + jnp.log(jnp.where(mine, 1.0, accum))
        high = level.astype(jnp.bfloat16).astype(jnp.float32)
        tail = jnp.where(lane % 64 < 32, high, level - high)
        return jnp.where(mine, mixed, tail).astype(jnp.bfloat16)

    def moved(part, group):
        rows = slice(group * SEG, group * SEG + SEG)
        return dot(place[part, :, rows], gathered[rows, :])

    for group in range(SEGS - 1):
        wait_bytes(recv1.at[pl.ds(8 * group, 8)], rsem1.at[group])

        def regroup(part, _, group=group):
            term = moved(part, group)
            at = pl.ds(pl.multiple_of(part * SEG, SEG), SEG)
            for cols in range(GROUPS):
                piece = term[:, lanes(cols)]
                xf[cols, at, :] = piece if group == 0 else xf[cols, at, :] + piece
            return 0

        @pl.when(head < HEADS)
        def _(group=group):
            far_project(group)
            if group == SEGS - 2:
                swap(0).start()

        lax.fori_loop(0, SEGS, regroup, 0)

    def deliver(part, _):
        term = moved(part, SEGS - 1)
        at = pl.ds(pl.multiple_of(part * SEG, SEG), SEG)
        for cols in range(GROUPS):
            piece = (xf[cols, at, :] + term[:, lanes(cols)]).astype(jnp.bfloat16)
            send2[part, :, :, lanes(cols)] = piece.reshape(SHARDS, 16, 128)

        def give(step, _):
            to = peer(me, step)
            pltpu.make_async_remote_copy(
                src_ref=send2.at[part, to], dst_ref=recv2.at[part, me],
                send_sem=ssem2.at[part], recv_sem=rsem2.at[part],
                device_id={"seq": to}, device_id_type=MESH,
            ).start()
            return 0

        lax.fori_loop(1, SHARDS, give, 0)
        pltpu.make_async_copy(send2.at[part, me], recv2.at[part, me], rsem2.at[part]).start()
        return 0

    wait_bytes(recv1.at[pl.ds(24, 8)], rsem1.at[SEGS - 1])

    def far(index, _):
        rows = pl.ds(pl.multiple_of(index * SEG, SEG), SEG)
        fout[rows, :] = far_result(*far_blocks(qf[rows, :]))
        return 0

    def return_far():
        def reorder(part, _):
            farsend[part] = dot(place[part], fout[...]).astype(jnp.bfloat16).reshape(
                SHARDS, 16, 128
            )
            return 0

        lax.fori_loop(0, SEGS, reorder, 0)

        def give_far(step, _):
            to = peer(me, step)
            pltpu.make_async_remote_copy(
                src_ref=farsend.at[:, to], dst_ref=farrecv.at[me], send_sem=fss, recv_sem=frs,
                device_id={"seq": to}, device_id_type=MESH,
            ).start()
            return 0

        lax.fori_loop(1, SHARDS, give_far, 0)
        pltpu.make_async_copy(farsend.at[:, me], farrecv.at[me], frs).start()

    def deliver_beside_far(part, _):
        deliver(part, 0)

        @pl.when(jnp.logical_and(head < HEADS, part < 2))
        def _():
            @pl.when(part == 0)
            def _():
                far_project(SEGS - 1)
                swap(1).start()
                swap(0).wait()
                swap(1).wait()

            lax.fori_loop(2 * part, 2 * part + 2, far, 0)
            pl.when(part == 1)(return_far)

        return 0

    lax.fori_loop(0, SEGS - 1, deliver_beside_far, 0)
    load_o.wait()
    low = iota((SEG, 128), 1) < HEAD_DIM
    low_far = iota((16, 128), 1) < HEAD_DIM

    wait_bytes(send1.at[pl.ds(0, SHARDS - 1)], ssem1)
    attn = send1.reshape(ROWS, WIDTH)
    encst = recv1.reshape(ROWS, WIDTH)

    def near_level(part):
        slot = lax.rem(part, 2)
        wait_bytes(recv2.at[part], rsem2.at[part])
        for at in range(0, SHARDS, 8):
            rows = recv2[part, at : at + 8].reshape(128, WIDTH).astype(jnp.float32)
            normed[16 * at : 16 * at + 128, :] = normalize(rows, gain)

        def project(index):
            for kind in range(3):
                cols = slice(kind * WIDTH + index * 256, kind * WIDTH + index * 256 + 256)
                qkv[:, cols] = dot(normed[...], wqkv[:, cols]).astype(jnp.bfloat16)

        def operands(number):
            pair, side = number // 2, number % 2
            mine = low if side == 0 else jnp.logical_not(low)
            queries = qkv[:, lanes(pair)] * jnp.bfloat16(score_scale)
            values = qkv[:, lanes(pair + 2 * PAIRS)]
            return (
                jnp.where(mine, queries, jnp.zeros_like(queries)),
                qkv[:, lanes(pair + PAIRS)],
                jnp.where(mine, values, jnp.ones_like(values)),
            )

        def start_head(number):
            queries, keys, values = operands(number)
            return dot_t(queries, keys), values

        project(0)
        upcoming = start_head(0)
        kept = []
        for number in range(HEADS):
            scores, values = upcoming
            if number % 4 == 0 and number + 4 < HEADS:
                project(number // 4 + 1)
            if number + 1 < HEADS:
                upcoming = start_head(number + 1)
            peak = jnp.max(scores, axis=-1, keepdims=True)
            weights = jnp.exp(scores - peak).astype(jnp.bfloat16)
            kept.append((dot(weights, values), peak))
            if number % 2:
                (accum0, peak0), (accum1, peak1) = kept
                kept = []
                total = pltpu.roll(jnp.where(low, accum1, accum0), 64, 1)
                pair = number // 2
                mix[slot, pair] = jnp.where(low, accum0, accum1) / total
                lse[slot, pair] = jnp.where(low, peak0, peak1) + jnp.log(total)

    def merge(part):
        slot = lax.rem(part, 2)
        for src in range(FAR_OWNERS):
            number = src // 2
            pair, half = number // 2, number % 2
            rows = slice(16 * src, 16 * src + 16)
            near_part = mix[slot, pair, rows, :]
            near_lse = lse[slot, pair, rows, :]
            far_part = farrecv[src, part].astype(jnp.float32)
            other = HEAD_DIM * (1 - half)
            far_lse = far_part[:, other : other + 1] + far_part[:, other + 32 : other + 33]
            top = jnp.maximum(near_lse, far_lse)
            near_share = jnp.exp(near_lse - top)
            far_share = jnp.exp(far_lse - top)
            mixed = (near_share * near_part + far_share * far_part) / (near_share + far_share)
            mine = low_far if half == 0 else jnp.logical_not(low_far)
            mix[slot, pair, rows, :] = jnp.where(mine, mixed, near_part)

        here = pl.ds(pl.multiple_of(part * SEG, SEG), SEG)
        for group in range(GROUPS):
            attn[here, lanes(group)] = mix[slot, group].astype(jnp.bfloat16)
        for index in range(3):
            cols = slice(index * 256, index * 256 + 256)
            term = lax.dot_general(
                attn[here, :], xb[here, cols], (((0,), (0,)), ((), ())),
                preferred_element_type=jnp.float32,
            )
            for sub in range(2):
                group = 2 * index + sub
                piece = term[:, lanes(sub)]
                grad[group] = jnp.where(part == 0, piece, grad[group] + piece)

    def segment(step, _):
        pl.when(step < SEGS)(functools.partial(near_level, step))

        @pl.when(step == 0)
        def _():
            deliver(SEGS - 1, 0)

        @pl.when(step == 1)
        def _():
            wait_bytes(farrecv, frs)

        pl.when(step > 0)(functools.partial(merge, step - 1))
        return 0

    def finish(part, _):
        here = pl.ds(pl.multiple_of(part * SEG, SEG), SEG)
        inputs = recv2[part].reshape(SEG, WIDTH)
        for index in range(3):
            cols = slice(index * 256, index * 256 + 256)
            projected = dot(attn[here, :], wout[:, cols])
            summed = (inputs[:, cols].astype(jnp.float32) + projected).astype(jnp.bfloat16)
            encst[here, cols] = dot(ordered[...], summed).astype(jnp.bfloat16)
        pltpu.make_async_copy(encst.at[here], enc_hbm.at[here], esem.at[part]).start()
        return 0

    lax.fori_loop(0, SEGS + 1, segment, 0)

    for side in range(2):
        for group in range(3):
            gsend[side, :, lanes(group)] = grad[3 * side + group].astype(jnp.bfloat16)
    join = pltpu.make_async_remote_copy(
        src_ref=gsend.at[1 - core], dst_ref=gmate, send_sem=jss, recv_sem=jrs,
        device_id={"seq": mate}, device_id_type=MESH,
    )
    join.start()
    lax.fori_loop(0, 2, finish, 0)
    join.wait()
    both = gsend[core].astype(jnp.float32) + gmate[...].astype(jnp.float32)
    gpart[...] = both.astype(jnp.bfloat16).reshape(SHARDS // 2, 48, 384)

    def give_grad(step, _):
        to = lax.rem(lax.div(me, 8) + lax.rem(step, 4), 4) * 8 + lax.rem(
            lax.rem(lax.div(me, 2), 4) + lax.rem(step + lax.div(step, 4), 4), 4
        ) * 2 + core
        pltpu.make_async_remote_copy(
            src_ref=gpart.at[lax.div(to, 2)], dst_ref=grecv.at[head], send_sem=gss, recv_sem=grs,
            device_id={"seq": to}, device_id_type=MESH,
        ).start()
        return 0

    lax.fori_loop(1, SHARDS // 2, give_grad, 0)
    pltpu.make_async_copy(gpart.at[head], grecv.at[head], grs).start()
    lax.fori_loop(2, SEGS, finish, 0)
    wait_bytes(grecv, grs)
    ysend[...] = jnp.sum(grecv[...].astype(jnp.float32), axis=0).astype(jnp.bfloat16)
    for step in range(1, SLIDES):
        pltpu.make_async_remote_copy(
            src_ref=ysend, dst_ref=yrecv.at[dp], send_sem=yss, recv_sem=yrs,
            device_id={"dp": lax.rem(dp + step, SLIDES)}, device_id_type=MESH,
        ).start()
    pltpu.make_async_copy(ysend, yrecv.at[dp], yrs).start()
    wait_bytes(yrecv, yrs)
    whole = jnp.sum(yrecv[...].astype(jnp.float32), axis=0)
    ysum[0] = whole[:24]
    ysum[1] = whole[24:]
    last = pltpu.make_async_remote_copy(
        src_ref=ysum.at[1 - core], dst_ref=fin.at[core], send_sem=css, recv_sem=crs,
        device_id={"seq": mate}, device_id_type=MESH,
    )
    last.start()
    fin[core] = ysum[core]
    last.wait()
    grad_ref[:, :384] = fin[0]
    grad_ref[:, 384:] = fin[1]

    wait_bytes(dall.at[pl.ds(0, SHARDS - 1)], dssem)
    for part in range(SEGS):
        wait_bytes(send2.at[part, pl.ds(0, SHARDS - 1)], ssem2.at[part])
        wait_bytes(encst.at[pl.ds(part * SEG, SEG)], esem.at[part])

    @pl.when(head < HEADS)
    def _():
        wait_bytes(farsend.at[:, pl.ds(0, SHARDS - 1)], fss)

    wait_bytes(gpart.at[pl.ds(0, SHARDS // 2 - 1)], gss)
    wait_bytes(yrecv.at[pl.ds(0, SLIDES - 1)], yss)


def body(tile_rows, block_dest, norm_gain, qkv_weight, out_weight, cotangent):
    bf16, f32 = jnp.bfloat16, jnp.float32
    dma = pltpu.SemaphoreType.DMA
    anywhere = pl.BlockSpec(memory_space=pl.ANY)
    vmem = pl.BlockSpec(memory_space=pltpu.VMEM)
    encoded, grad = pl.pallas_call(
        kernel,
        out_shape=(
            jax.ShapeDtypeStruct((ROWS, WIDTH), bf16),
            jax.ShapeDtypeStruct((24, WIDTH), f32),
        ),
        in_specs=[anywhere, vmem, vmem, anywhere, anywhere, anywhere],
        out_specs=(anywhere, vmem),
        scratch_shapes=[
            pltpu.VMEM((ROWS, WIDTH), bf16),
            pltpu.VMEM((GROUPS, ROWS, 128), f32),
            pltpu.VMEM((SHARDS, 64, WIDTH), bf16),
            pltpu.VMEM((SHARDS, 64, WIDTH), bf16),
            pltpu.VMEM((8, 128), jnp.int32),
            pltpu.VMEM((SHARDS, 8, 128), jnp.int32),
            pltpu.VMEM((SEGS, SHARDS, 16, WIDTH), bf16),
            pltpu.VMEM((SEGS, SHARDS, 16, WIDTH), bf16),
            pltpu.VMEM((SEGS, SEG, ROWS), bf16),
            pltpu.VMEM((SEG, SEG), bf16),
            pltpu.VMEM((SEG, SEG), bf16),
            pltpu.VMEM((2, 2, ROWS, 128), bf16),
            pltpu.VMEM((ROWS, 128), bf16),
            pltpu.VMEM((ROWS, 128), bf16),
            pltpu.VMEM((SEGS, SHARDS, 16, 128), bf16),
            pltpu.VMEM((FAR_OWNERS, SEGS, 16, 128), bf16),
            pltpu.VMEM((WIDTH, 3 * WIDTH), bf16),
            pltpu.VMEM((WIDTH, 384), bf16),
            pltpu.VMEM((WIDTH, WIDTH), bf16),
            pltpu.VMEM((SEG, WIDTH), bf16),
            pltpu.VMEM((SEG, 3 * WIDTH), bf16),
            pltpu.VMEM((2, PAIRS, SEG, 128), f32),
            pltpu.VMEM((2, PAIRS, SEG, 128), f32),
            pltpu.VMEM((GROUPS, WIDTH, 128), f32),
            pltpu.VMEM((2, WIDTH, 384), bf16),
            pltpu.VMEM((WIDTH, 384), bf16),
            pltpu.VMEM((SHARDS // 2, 48, 384), bf16),
            pltpu.VMEM((SHARDS // 2, 48, 384), bf16),
            pltpu.VMEM((48, 384), bf16),
            pltpu.VMEM((SLIDES, 48, 384), bf16),
            pltpu.VMEM((2, 24, 384), f32),
            pltpu.VMEM((2, 24, 384), f32),
            dma, dma((SEGS,)), dma, dma, dma((SEGS,)), dma((SEGS,)), dma((2,)), dma((2,)),
            dma, dma, dma, dma, dma, dma, dma, dma, dma, dma,
            dma((SEGS,)), dma, dma, dma, dma((SEGS,)),
        ],
        compiler_params=pltpu.CompilerParams(
            collective_id=0, has_side_effects=True, vmem_limit_bytes=62 * 1024 * 1024
        ),
        name="slide_layer",
    )(
        tile_rows.reshape(ROWS, WIDTH), block_dest, norm_gain,
        qkv_weight, out_weight, cotangent.reshape(ROWS, WIDTH),
    )
    return encoded.reshape(1, ROWS, WIDTH), grad


def solution(mesh):
    return jax.shard_map(
        body,
        mesh=mesh,
        in_specs=(P("dp", "seq", None), P("dp", "seq"), P(), P(), P(), P("dp", "seq", None)),
        out_specs=(P("dp", "seq", None), P("seq", None)),
        check_vma=False,
    )
```

```python
import functools

import jax
import jax.numpy as jnp
from jax import lax
from jax.experimental import pallas as pl
from jax.experimental.pallas import tpu as pltpu
from jax.sharding import PartitionSpec as P

WIDTH = 768
HEADS = 12
HEAD_DIM = 64
BLK = 128
SEG = 512
RATE = 16
ROWS = 2048
SHARDS = 32
SLIDES = 4
SEGS = ROWS // SEG
STRIDE = 32
PAIRS = HEADS // 2
GROUPS = WIDTH // 128
FAR_OWNERS = 2 * HEADS
MESH = pl.DeviceIdType.MESH

score_scale = 0.125
norm_eps = 1e-06


def lanes(group):
    return slice(128 * group, 128 * group + 128)


def row_class(shard):
    return RATE * lax.rem(shard, 2) + lax.div(shard, 2)


def peer(me, step):
    z, x, c = lax.div(me, 8), lax.rem(lax.div(me, 2), 4), lax.rem(me, 2)
    dz = lax.rem(step, 4)
    dx = lax.rem(step + lax.div(step, 8), 4)
    dc = lax.rem(lax.div(step, 4), 2)
    return lax.rem(z + dz, 4) * 8 + lax.rem(x + dx, 4) * 2 + lax.rem(c + dc, 2)


def origin(me, step):
    z, x, c = lax.div(me, 8), lax.rem(lax.div(me, 2), 4), lax.rem(me, 2)
    dz = lax.rem(step, 4)
    dx = lax.rem(step + lax.div(step, 8), 4)
    dc = lax.rem(lax.div(step, 4), 2)
    return lax.rem(z + 4 - dz, 4) * 8 + lax.rem(x + 4 - dx, 4) * 2 + lax.rem(c + 2 - dc, 2)


def normalize(values, gain):
    center = values - jnp.mean(values, axis=-1, keepdims=True)
    spread = jnp.mean(center * center, axis=-1, keepdims=True)
    return (center * lax.rsqrt(spread + norm_eps) * gain).astype(jnp.bfloat16)


def dot(a, b):
    return jnp.dot(a, b, preferred_element_type=jnp.float32)


def dot_t(a, b):
    return lax.dot_general(a, b, (((1,), (1,)), ((), ())), preferred_element_type=jnp.float32)


def iota(shape, dim):
    return lax.broadcasted_iota(jnp.int32, shape, dim)


def one_hot(mask):
    return jnp.where(mask, 1.0, 0.0).astype(jnp.bfloat16)


def wait_bytes(ref, sem):
    pltpu.make_async_copy(ref, ref, sem).wait()


def target_rows(me, dest_rows):
    dests = dest_rows.astype(jnp.bfloat16)
    spread = one_hot(iota((128, ROWS), 0) == iota((128, ROWS), 1) % 64)
    wide = dot(dests, spread)
    of_source = iota((SHARDS, ROWS), 0) == iota((SHARDS, ROWS), 1) // 64
    dest = jnp.sum(jnp.where(of_source, wide, 0.0), axis=0, keepdims=True)
    dest_int = dest.astype(jnp.int32)
    named = jnp.where(iota((SHARDS, ROWS), 0) == dest_int, 1.0, 0.0)
    row = iota((ROWS, 128), 0)
    first = one_hot(jnp.logical_and(row // 64 == iota((ROWS, 128), 1), row % 4 == 0))
    has = dot(named.astype(jnp.bfloat16), first)
    earlier = one_hot(origin(me, iota((128, 128), 0)) < origin(me, iota((128, 128), 1)))
    rank = dot(has.astype(jnp.bfloat16), earlier)
    back = one_hot(iota((128, ROWS), 0) == iota((128, ROWS), 1) // 64)
    rank_wide = dot(rank.astype(jnp.bfloat16), back)
    slot = jnp.sum(named * rank_wide, axis=0, keepdims=True).astype(jnp.int32)
    within = iota((1, ROWS), 1) % 4
    return (slot // 4) * SEG + dest_int * 16 + (slot % 4) * 4 + within


def kernel(
    x_hbm, dest_ref, gain_ref, wqkv_hbm, wout_hbm, cot_hbm, enc_hbm, grad_ref,
    xb, send1, recv1, dsend, dall, send2, recv2, place, ordered, classed, kv, qf, fout, farsend, farrecv,
    wqkv, wfar, wout, normed, qkv, mix, lse, grad, gsend, gmate, gpart, grecv, ysend, yrecv,
    ssem1, rsem1, dssem, drsem, ssem2, rsem2, kvs, kvr, fss, frs,
    jss, jrs, gss, grs, yss, yrs, xsem, wsem, osem, csem, esem,
):
    me = lax.axis_index("seq")
    dp = lax.axis_index("dp")
    core = lax.rem(me, 2)
    mate = me + 1 - 2 * core
    head = lax.div(me, 2)

    load_x = [
        pltpu.make_async_copy(
            x_hbm.at[pl.ds(at, SEG)], xb.at[pl.ds(at, SEG)], xsem.at[at // SEG]
        )
        for at in range(0, ROWS, SEG)
    ]
    for load in load_x:
        load.start()
    load_w = pltpu.make_async_copy(wqkv_hbm, wqkv, wsem)
    load_w.start()
    load_o = pltpu.make_async_copy(wout_hbm, wout, osem)
    load_o.start()

    barrier = pltpu.get_barrier_semaphore()

    def greet(step, _):
        pl.semaphore_signal(
            barrier, inc=1, device_id={"seq": peer(me, step)}, device_id_type=MESH
        )
        return 0

    lax.fori_loop(1, SHARDS, greet, 0)
    for step in range(1, SLIDES):
        for across in range(2):
            pl.semaphore_signal(
                barrier, inc=1,
                device_id={
                    "dp": lax.rem(dp + step, SLIDES),
                    "seq": me - core + lax.rem(core + across, 2),
                },
                device_id_type=MESH,
            )

    spread = one_hot(iota((16, 128), 0) == iota((16, 128), 1) // 4)
    dests = dot(dest_ref[...].astype(jnp.float32).astype(jnp.bfloat16), spread)
    dsend[...] = jnp.broadcast_to(dests, (8, 128)).astype(jnp.int32)

    row, col = iota((SEG, SEG), 0), iota((SEG, SEG), 1)
    classed[...] = one_hot(col == STRIDE * (row % 16) + row_class(row // 16))

    def pack(index, _):
        wait_bytes(xb.at[pl.ds(0, SEG)], xsem.at[index])
        rows = pl.ds(pl.multiple_of(index * SEG, SEG), SEG)
        found = dot(classed[...], xb[rows, :]).astype(jnp.bfloat16)
        to_rows = pl.ds(pl.multiple_of(index * 16, 16), 16)
        send1[:, to_rows, :] = found.reshape(SHARDS, 16, WIDTH)
        return 0

    lax.fori_loop(0, SEGS, pack, 0)
    load_c = pltpu.make_async_copy(cot_hbm, xb, csem)
    load_c.start()
    pl.semaphore_wait(barrier, SHARDS - 1 + 2 * (SLIDES - 1))

    def scatter(step, _):
        to = peer(me, step)
        pltpu.make_async_remote_copy(
            src_ref=send1.at[to], dst_ref=recv1.at[step], send_sem=ssem1,
            recv_sem=rsem1.at[lax.div(step, 8)],
            device_id={"seq": to}, device_id_type=MESH,
        ).start()
        return 0

    def tell(step, _):
        to = peer(me, step)
        pltpu.make_async_remote_copy(
            src_ref=dsend, dst_ref=dall.at[step], send_sem=dssem, recv_sem=drsem,
            device_id={"seq": to}, device_id_type=MESH,
        ).start()
        return 0

    lax.fori_loop(1, 8, scatter, 0)
    lax.fori_loop(1, SHARDS, tell, 0)
    pltpu.make_async_copy(dsend, dall.at[0], drsem).start()
    lax.fori_loop(8, SHARDS, scatter, 0)
    pltpu.make_async_copy(send1.at[me], recv1.at[0], rsem1.at[0]).start()

    wait_bytes(dall, drsem)
    target = target_rows(me, jnp.max(dall[...].astype(jnp.float32), axis=1))

    def build(part, _):
        rows = iota((SEG, ROWS), 0) + part * SEG
        place[part] = one_hot(rows == target)
        return 0

    lax.fori_loop(0, SEGS, build, 0)
    ordered[...] = one_hot(col == 32 * (row % RATE) + 16 * (row % STRIDE // RATE) + row // STRIDE)
    load_c.wait()

    def class_order(part, _):
        rows = pl.ds(pl.multiple_of(part * SEG, SEG), SEG)
        xb[rows, :] = dot(classed[...], xb[rows, :]).astype(jnp.bfloat16)
        return 0

    lax.fori_loop(0, SEGS, class_order, 0)
    load_w.wait()
    pair_at = lax.div(head, 2) * 128
    for part in range(3):
        at = pl.multiple_of(jnp.minimum(pair_at, WIDTH - 128) + part * WIDTH, 128)
        wfar[:, part * 128 : (part + 1) * 128] = wqkv[:, pl.ds(at, 128)]

    gathered = recv1.reshape(ROWS, WIDTH)
    gain = gain_ref[...].reshape(1, WIDTH)
    half = lax.rem(head, 2)

    def far_project(group):
        mine = iota((SEG, 128), 1) // HEAD_DIM == half
        rows = slice(group * SEG, group * SEG + SEG)
        out = dot(normalize(gathered[rows, :].astype(jnp.float32), gain), wfar[...])
        out = out.astype(jnp.bfloat16)
        zero, one = jnp.bfloat16(0.0), jnp.bfloat16(1.0)
        qf[rows, :] = jnp.where(mine, out[:, :128] * jnp.bfloat16(score_scale), zero)
        kv[core, 0, rows, :] = out[:, 128:256]
        kv[core, 1, rows, :] = jnp.where(mine, out[:, 256:], one)

    def swap(stage):
        rows = pl.ds(stage * 3 * SEG, 3 * SEG if stage == 0 else SEG)
        return pltpu.make_async_remote_copy(
            src_ref=kv.at[core, :, rows], dst_ref=kv.at[core, :, rows],
            send_sem=kvs.at[stage], recv_sem=kvr.at[stage],
            device_id={"seq": mate}, device_id_type=MESH,
        )

    blocks = [(side, slice(at, at + SEG)) for side in range(2) for at in range(0, ROWS, SEG)]

    def far_blocks(queries):
        accum = peak = None
        upcoming = dot_t(queries, kv[blocks[0][0], 0, blocks[0][1], :])
        for number, (side, keys) in enumerate(blocks):
            scores = upcoming
            if number + 1 < len(blocks):
                after, cut = blocks[number + 1]
                upcoming = dot_t(queries, kv[after, 0, cut, :])
            top = jnp.max(scores, axis=-1, keepdims=True)
            if peak is not None:
                top = jnp.maximum(peak, top)
                accum = accum * jnp.exp(peak - top)
            term = dot(jnp.exp(scores - top).astype(jnp.bfloat16), kv[side, 1, keys, :])
            accum = term if accum is None else accum + term
            peak = top
        return accum, peak

    def far_result(accum, peak):
        lane = iota((SEG, 128), 1)
        mine = lane // HEAD_DIM == half
        mixed = accum / pltpu.roll(accum, 64, 1)
        level = peak + jnp.log(jnp.where(mine, 1.0, accum))
        high = level.astype(jnp.bfloat16).astype(jnp.float32)
        tail = jnp.where(lane % 64 < 32, high, level - high)
        return jnp.where(mine, mixed, tail).astype(jnp.bfloat16)

    def moved(part, group):
        rows = slice(group * SEG, group * SEG + SEG)
        found = dot(place[part, :, rows], gathered[rows, :]).astype(jnp.bfloat16)
        return found.reshape(SHARDS, 16, WIDTH)

    for group in range(SEGS - 1):
        wait_bytes(recv1.at[pl.ds(8 * group, 8)], rsem1.at[group])

        def regroup(part, _, group=group):
            term = moved(part, group)
            send2[part] = term if group == 0 else send2[part] + term
            return 0

        @pl.when(head < HEADS)
        def _(group=group):
            far_project(group)
            if group == SEGS - 2:
                swap(0).start()

        lax.fori_loop(0, SEGS, regroup, 0)

    def deliver(part, _):
        send2[part] = send2[part] + moved(part, SEGS - 1)

        def give(step, _):
            to = peer(me, step)
            pltpu.make_async_remote_copy(
                src_ref=send2.at[part, to], dst_ref=recv2.at[part, me],
                send_sem=ssem2.at[part], recv_sem=rsem2.at[part],
                device_id={"seq": to}, device_id_type=MESH,
            ).start()
            return 0

        lax.fori_loop(1, SHARDS, give, 0)
        pltpu.make_async_copy(send2.at[part, me], recv2.at[part, me], rsem2.at[part]).start()
        return 0

    wait_bytes(recv1.at[pl.ds(24, 8)], rsem1.at[SEGS - 1])

    def far(index, _):
        rows = pl.ds(pl.multiple_of(index * SEG, SEG), SEG)
        fout[rows, :] = far_result(*far_blocks(qf[rows, :]))
        return 0

    def return_far():
        def reorder(part, _):
            farsend[part] = dot(place[part], fout[...]).astype(jnp.bfloat16).reshape(
                SHARDS, 16, 128
            )
            return 0

        lax.fori_loop(0, SEGS, reorder, 0)

        def give_far(step, _):
            to = peer(me, step)
            pltpu.make_async_remote_copy(
                src_ref=farsend.at[:, to], dst_ref=farrecv.at[me], send_sem=fss, recv_sem=frs,
                device_id={"seq": to}, device_id_type=MESH,
            ).start()
            return 0

        lax.fori_loop(1, SHARDS, give_far, 0)
        pltpu.make_async_copy(farsend.at[:, me], farrecv.at[me], frs).start()

    def deliver_beside_far(part, _):
        deliver(part, 0)

        @pl.when(jnp.logical_and(head < HEADS, part == 0))
        def _():
            far_project(SEGS - 1)
            swap(1).start()

        @pl.when(jnp.logical_and(head < HEADS, jnp.logical_or(part == 1, part == 2)))
        def _():
            @pl.when(part == 1)
            def _():
                swap(0).wait()
                swap(1).wait()

            lax.fori_loop(2 * part - 2, 2 * part, far, 0)
            pl.when(part == 2)(return_far)

        return 0

    lax.fori_loop(0, SEGS, deliver_beside_far, 0)
    load_o.wait()
    low = iota((SEG, 128), 1) < HEAD_DIM
    low_far = iota((16, 128), 1) < HEAD_DIM

    wait_bytes(send1.at[pl.ds(0, SHARDS - 1)], ssem1)
    attn = send1.reshape(ROWS, WIDTH)
    encst = recv1.reshape(ROWS, WIDTH)

    def near_level(part):
        slot = lax.rem(part, 2)
        wait_bytes(recv2.at[part], rsem2.at[part])
        for at in range(0, SHARDS, 8):
            rows = recv2[part, at : at + 8].reshape(128, WIDTH).astype(jnp.float32)
            normed[16 * at : 16 * at + 128, :] = normalize(rows, gain)

        def project(index):
            for kind in range(3):
                cols = slice(kind * WIDTH + index * 256, kind * WIDTH + index * 256 + 256)
                qkv[:, cols] = dot(normed[...], wqkv[:, cols]).astype(jnp.bfloat16)

        def operands(number):
            pair, side = number // 2, number % 2
            mine = low if side == 0 else jnp.logical_not(low)
            queries = qkv[:, lanes(pair)] * jnp.bfloat16(score_scale)
            values = qkv[:, lanes(pair + 2 * PAIRS)]
            return (
                jnp.where(mine, queries, jnp.zeros_like(queries)),
                qkv[:, lanes(pair + PAIRS)],
                jnp.where(mine, values, jnp.ones_like(values)),
            )

        def start_head(number):
            queries, keys, values = operands(number)
            return dot_t(queries, keys), values

        project(0)
        upcoming = start_head(0)
        kept = []
        for number in range(HEADS):
            scores, values = upcoming
            if number % 4 == 0 and number + 4 < HEADS:
                project(number // 4 + 1)
            if number + 1 < HEADS:
                upcoming = start_head(number + 1)
            peak = jnp.max(scores, axis=-1, keepdims=True)
            weights = jnp.exp(scores - peak).astype(jnp.bfloat16)
            kept.append((dot(weights, values), peak))
            if number % 2:
                (accum0, peak0), (accum1, peak1) = kept
                kept = []
                total = pltpu.roll(jnp.where(low, accum1, accum0), 64, 1)
                pair = number // 2
                mix[slot, pair] = jnp.where(low, accum0, accum1) / total
                lse[slot, pair] = jnp.where(low, peak0, peak1) + jnp.log(total)

    def merge(part):
        slot = lax.rem(part, 2)
        for src in range(FAR_OWNERS):
            number = src // 2
            pair, half = number // 2, number % 2
            rows = slice(16 * src, 16 * src + 16)
            near_part = mix[slot, pair, rows, :]
            near_lse = lse[slot, pair, rows, :]
            far_part = farrecv[src, part].astype(jnp.float32)
            other = HEAD_DIM * (1 - half)
            far_lse = far_part[:, other : other + 1] + far_part[:, other + 32 : other + 33]
            top = jnp.maximum(near_lse, far_lse)
            near_share = jnp.exp(near_lse - top)
            far_share = jnp.exp(far_lse - top)
            mixed = (near_share * near_part + far_share * far_part) / (near_share + far_share)
            mine = low_far if half == 0 else jnp.logical_not(low_far)
            mix[slot, pair, rows, :] = jnp.where(mine, mixed, near_part)

        here = pl.ds(pl.multiple_of(part * SEG, SEG), SEG)
        for group in range(GROUPS):
            attn[here, lanes(group)] = mix[slot, group].astype(jnp.bfloat16)
        for index in range(3):
            cols = slice(index * 256, index * 256 + 256)
            term = lax.dot_general(
                attn[here, :], xb[here, cols], (((0,), (0,)), ((), ())),
                preferred_element_type=jnp.float32,
            )
            for sub in range(2):
                group = 2 * index + sub
                piece = term[:, lanes(sub)]
                grad[group] = jnp.where(part == 0, piece, grad[group] + piece)

    def segment(step, _):
        pl.when(step < SEGS)(functools.partial(near_level, step))

        @pl.when(step == 1)
        def _():
            wait_bytes(farrecv, frs)

        pl.when(step > 0)(functools.partial(merge, step - 1))
        return 0

    def finish(part, _):
        here = pl.ds(pl.multiple_of(part * SEG, SEG), SEG)
        inputs = recv2[part].reshape(SEG, WIDTH)
        for index in range(3):
            cols = slice(index * 256, index * 256 + 256)
            projected = dot(attn[here, :], wout[:, cols])
            summed = (inputs[:, cols].astype(jnp.float32) + projected).astype(jnp.bfloat16)
            encst[here, cols] = dot(ordered[...], summed).astype(jnp.bfloat16)
        pltpu.make_async_copy(encst.at[here], enc_hbm.at[here], esem.at[part]).start()
        return 0

    lax.fori_loop(0, SEGS + 1, segment, 0)

    def cast_grad(side):
        for group in range(3):
            gsend[side, :, lanes(group)] = grad[3 * side + group].astype(jnp.bfloat16)

    cast_grad(1 - core)
    join = pltpu.make_async_remote_copy(
        src_ref=gsend.at[1 - core], dst_ref=gmate, send_sem=jss, recv_sem=jrs,
        device_id={"seq": mate}, device_id_type=MESH,
    )
    join.start()
    cast_grad(core)
    finish(0, 0)
    join.wait()
    both = gsend[core].astype(jnp.float32) + gmate[...].astype(jnp.float32)
    gpart[...] = both.astype(jnp.bfloat16).reshape(SHARDS // 2, 48, 384)

    def give_grad(step, _):
        to = lax.rem(lax.div(me, 8) + lax.rem(step, 4), 4) * 8 + lax.rem(
            lax.rem(lax.div(me, 2), 4) + lax.rem(step + lax.div(step, 4), 4), 4
        ) * 2 + core
        pltpu.make_async_remote_copy(
            src_ref=gpart.at[lax.div(to, 2)], dst_ref=grecv.at[head], send_sem=gss, recv_sem=grs,
            device_id={"seq": to}, device_id_type=MESH,
        ).start()
        return 0

    lax.fori_loop(1, SHARDS // 2, give_grad, 0)
    pltpu.make_async_copy(gpart.at[head], grecv.at[head], grs).start()
    lax.fori_loop(1, SEGS, finish, 0)
    wait_bytes(grecv, grs)
    summed = jnp.sum(grecv[...].astype(jnp.float32), axis=0)
    ysend[0] = summed[:24]
    ysend[1] = summed[24:]
    for step in range(SLIDES):
        for across in range(2):
            side = lax.rem(core + across, 2)
            landing = yrecv.at[core, dp]
            if step or across:
                pltpu.make_async_remote_copy(
                    src_ref=ysend.at[side], dst_ref=landing, send_sem=yss, recv_sem=yrs,
                    device_id={"dp": lax.rem(dp + step, SLIDES), "seq": me - core + side},
                    device_id_type=MESH,
                ).start()
            else:
                pltpu.make_async_copy(ysend.at[side], landing, yrs).start()
    wait_bytes(yrecv, yrs)
    for side in range(2):
        total = (yrecv[side, 0] + yrecv[side, 1]) + (yrecv[side, 2] + yrecv[side, 3])
        grad_ref[:, 384 * side : 384 * side + 384] = total

    wait_bytes(dall.at[pl.ds(0, SHARDS - 1)], dssem)
    for part in range(SEGS):
        wait_bytes(send2.at[part, pl.ds(0, SHARDS - 1)], ssem2.at[part])
        wait_bytes(encst.at[pl.ds(part * SEG, SEG)], esem.at[part])

    @pl.when(head < HEADS)
    def _():
        wait_bytes(farsend.at[:, pl.ds(0, SHARDS - 1)], fss)

    wait_bytes(gpart.at[pl.ds(0, SHARDS // 2 - 1)], gss)
    wait_bytes(yrecv.at[0], yss)
    wait_bytes(yrecv.at[1, pl.ds(0, SLIDES - 1)], yss)


def hand_on(src, dst, held, in_sems, out_sems):
    pieces = [pl.ds(at, SEG) for at in range(0, ROWS, SEG)]
    into = [
        pltpu.make_async_copy(src.at[rows], held.at[rows], in_sems.at[number])
        for number, rows in enumerate(pieces)
    ]
    out = [
        pltpu.make_async_copy(held.at[rows], dst.at[rows], out_sems.at[number])
        for number, rows in enumerate(pieces)
    ]
    for copy in into:
        copy.start()
    for first, second in zip(into, out):
        first.wait()
        second.start()
    for copy in out:
        copy.wait()


def body(tile_rows, block_dest, norm_gain, qkv_weight, out_weight, cotangent):
    bf16, f32 = jnp.bfloat16, jnp.float32
    dma = pltpu.SemaphoreType.DMA
    anywhere = pl.BlockSpec(memory_space=pl.ANY)
    vmem = pl.BlockSpec(memory_space=pltpu.VMEM)
    encoded, grad = pl.pallas_call(
        kernel,
        out_shape=(
            jax.ShapeDtypeStruct((ROWS, WIDTH), bf16),
            jax.ShapeDtypeStruct((24, WIDTH), f32),
        ),
        in_specs=[anywhere, vmem, vmem, anywhere, anywhere, anywhere],
        out_specs=(anywhere, vmem),
        scratch_shapes=[
            pltpu.VMEM((ROWS, WIDTH), bf16),
            pltpu.VMEM((SHARDS, 64, WIDTH), bf16),
            pltpu.VMEM((SHARDS, 64, WIDTH), bf16),
            pltpu.VMEM((8, 128), jnp.int32),
            pltpu.VMEM((SHARDS, 8, 128), jnp.int32),
            pltpu.VMEM((SEGS, SHARDS, 16, WIDTH), bf16),
            pltpu.VMEM((SEGS, SHARDS, 16, WIDTH), bf16),
            pltpu.VMEM((SEGS, SEG, ROWS), bf16),
            pltpu.VMEM((SEG, SEG), bf16),
            pltpu.VMEM((SEG, SEG), bf16),
            pltpu.VMEM((2, 2, ROWS, 128), bf16),
            pltpu.VMEM((ROWS, 128), bf16),
            pltpu.VMEM((ROWS, 128), bf16),
            pltpu.VMEM((SEGS, SHARDS, 16, 128), bf16),
            pltpu.VMEM((FAR_OWNERS, SEGS, 16, 128), bf16),
            pltpu.VMEM((WIDTH, 3 * WIDTH), bf16),
            pltpu.VMEM((WIDTH, 384), bf16),
            pltpu.VMEM((WIDTH, WIDTH), bf16),
            pltpu.VMEM((SEG, WIDTH), bf16),
            pltpu.VMEM((SEG, 3 * WIDTH), bf16),
            pltpu.VMEM((2, PAIRS, SEG, 128), f32),
            pltpu.VMEM((2, PAIRS, SEG, 128), f32),
            pltpu.VMEM((GROUPS, WIDTH, 128), f32),
            pltpu.VMEM((2, WIDTH, 384), bf16),
            pltpu.VMEM((WIDTH, 384), bf16),
            pltpu.VMEM((SHARDS // 2, 48, 384), bf16),
            pltpu.VMEM((SHARDS // 2, 48, 384), bf16),
            pltpu.VMEM((2, 24, 384), f32),
            pltpu.VMEM((2, SLIDES, 24, 384), f32),
            dma, dma((SEGS,)), dma, dma, dma((SEGS,)), dma((SEGS,)), dma((2,)), dma((2,)),
            dma, dma, dma, dma, dma, dma, dma, dma,
            dma((SEGS,)), dma, dma, dma, dma((SEGS,)),
        ],
        compiler_params=pltpu.CompilerParams(
            collective_id=0, has_side_effects=True, vmem_limit_bytes=62 * 1024 * 1024
        ),
        name="slide_layer",
    )(
        tile_rows.reshape(ROWS, WIDTH), block_dest, norm_gain,
        qkv_weight, out_weight, cotangent.reshape(ROWS, WIDTH),
    )
    encoded = pl.pallas_call(
        hand_on,
        out_shape=jax.ShapeDtypeStruct((ROWS, WIDTH), bf16),
        in_specs=[anywhere],
        out_specs=anywhere,
        scratch_shapes=[pltpu.VMEM((ROWS, WIDTH), bf16), dma((SEGS,)), dma((SEGS,))],
        name="hand_on",
    )(encoded)
    return encoded.reshape(1, ROWS, WIDTH), grad


def solution(mesh):
    return jax.shard_map(
        body,
        mesh=mesh,
        in_specs=(P("dp", "seq", None), P("dp", "seq"), P(), P(), P(), P("dp", "seq", None)),
        out_specs=(P("dp", "seq", None), P("seq", None)),
        check_vma=False,
    )
```

```python
import functools

import jax
import jax.numpy as jnp
from jax import lax
from jax.experimental import pallas as pl
from jax.experimental.pallas import tpu as pltpu
from jax.sharding import PartitionSpec as P

WIDTH = 768
HEADS = 12
HEAD_DIM = 64
BLK = 128
SEG = 512
RATE = 16
ROWS = 2048
SHARDS = 32
SLIDES = 4
SEGS = ROWS // SEG
STRIDE = 32
PAIRS = HEADS // 2
GROUPS = WIDTH // 128
FAR_OWNERS = 2 * HEADS
MESH = pl.DeviceIdType.MESH

score_scale = 0.125
norm_eps = 1e-06


def lanes(group):
    return slice(128 * group, 128 * group + 128)


def row_class(shard):
    return RATE * lax.rem(shard, 2) + lax.div(shard, 2)


def peer(me, step):
    z, x, c = lax.div(me, 8), lax.rem(lax.div(me, 2), 4), lax.rem(me, 2)
    dz = lax.rem(step, 4)
    dx = lax.rem(step + lax.rem(lax.div(step, 4), 4), 4)
    dc = lax.div(step, 16)
    return lax.rem(z + dz, 4) * 8 + lax.rem(x + dx, 4) * 2 + lax.rem(c + dc, 2)


def origin(me, step):
    z, x, c = lax.div(me, 8), lax.rem(lax.div(me, 2), 4), lax.rem(me, 2)
    dz = lax.rem(step, 4)
    dx = lax.rem(step + lax.rem(lax.div(step, 4), 4), 4)
    dc = lax.div(step, 16)
    return lax.rem(z + 4 - dz, 4) * 8 + lax.rem(x + 4 - dx, 4) * 2 + lax.rem(c + 2 - dc, 2)


def normalize(values, gain):
    center = values - jnp.mean(values, axis=-1, keepdims=True)
    spread = jnp.mean(center * center, axis=-1, keepdims=True)
    return (center * lax.rsqrt(spread + norm_eps) * gain).astype(jnp.bfloat16)


def dot(a, b):
    return jnp.dot(a, b, preferred_element_type=jnp.float32)


def dot_t(a, b):
    return lax.dot_general(a, b, (((1,), (1,)), ((), ())), preferred_element_type=jnp.float32)


def iota(shape, dim):
    return lax.broadcasted_iota(jnp.int32, shape, dim)


def one_hot(mask):
    return jnp.where(mask, 1.0, 0.0).astype(jnp.bfloat16)


def wait_bytes(ref, sem):
    pltpu.make_async_copy(ref, ref, sem).wait()


def target_rows(me, dest_rows):
    dests = dest_rows.astype(jnp.bfloat16)
    spread = one_hot(iota((128, ROWS), 0) == iota((128, ROWS), 1) % 64)
    wide = dot(dests, spread)
    of_source = iota((SHARDS, ROWS), 0) == iota((SHARDS, ROWS), 1) // 64
    dest = jnp.sum(jnp.where(of_source, wide, 0.0), axis=0, keepdims=True)
    dest_int = dest.astype(jnp.int32)
    named = jnp.where(iota((SHARDS, ROWS), 0) == dest_int, 1.0, 0.0)
    row = iota((ROWS, 128), 0)
    first = one_hot(jnp.logical_and(row // 64 == iota((ROWS, 128), 1), row % 4 == 0))
    has = dot(named.astype(jnp.bfloat16), first)
    earlier = one_hot(origin(me, iota((128, 128), 0)) < origin(me, iota((128, 128), 1)))
    rank = dot(has.astype(jnp.bfloat16), earlier)
    back = one_hot(iota((128, ROWS), 0) == iota((128, ROWS), 1) // 64)
    rank_wide = dot(rank.astype(jnp.bfloat16), back)
    slot = jnp.sum(named * rank_wide, axis=0, keepdims=True).astype(jnp.int32)
    within = iota((1, ROWS), 1) % 4
    return (slot // 4) * SEG + dest_int * 16 + (slot % 4) * 4 + within


def kernel(
    x_hbm, dest_ref, gain_ref, wqkv_hbm, wout_hbm, cot_hbm, enc_hbm, grad_ref,
    xb, send1, recv1, dsend, dall, send2, recv2, place, ordered, classed, kv, qf, fout, farsend, farrecv,
    wqkv, wfar, wout, normed, qkv, mix, lse, grad, gsend, gmate, gpart, grecv, ysend, yrecv,
    ssem1, rsem1, dssem, drsem, ssem2, rsem2, kvs, kvr, fss, frs,
    jss, jrs, gss, grs, yss, yrs, xsem, wsem, osem, csem, esem,
):
    me = lax.axis_index("seq")
    dp = lax.axis_index("dp")
    core = lax.rem(me, 2)
    mate = me + 1 - 2 * core
    head = lax.div(me, 2)

    load_x = [
        pltpu.make_async_copy(
            x_hbm.at[pl.ds(at, SEG)], xb.at[pl.ds(at, SEG)], xsem.at[at // SEG]
        )
        for at in range(0, ROWS, SEG)
    ]
    for load in load_x:
        load.start()
    load_w = pltpu.make_async_copy(wqkv_hbm, wqkv, wsem)
    load_w.start()
    load_o = pltpu.make_async_copy(wout_hbm, wout, osem)
    load_o.start()

    barrier = pltpu.get_barrier_semaphore()

    def greet(step, _):
        pl.semaphore_signal(
            barrier, inc=1, device_id={"seq": peer(me, step)}, device_id_type=MESH
        )
        return 0

    lax.fori_loop(1, SHARDS, greet, 0)
    for step in range(1, SLIDES):
        for across in range(2):
            pl.semaphore_signal(
                barrier, inc=1,
                device_id={
                    "dp": lax.rem(dp + step, SLIDES),
                    "seq": me - core + lax.rem(core + across, 2),
                },
                device_id_type=MESH,
            )

    spread = one_hot(iota((16, 128), 0) == iota((16, 128), 1) // 4)
    dests = dot(dest_ref[...].astype(jnp.float32).astype(jnp.bfloat16), spread)
    dsend[...] = jnp.broadcast_to(dests, (8, 128)).astype(jnp.int32)

    row, col = iota((SEG, SEG), 0), iota((SEG, SEG), 1)
    classed[...] = one_hot(col == STRIDE * (row % 16) + row_class(row // 16))

    def pack(index, _):
        wait_bytes(xb.at[pl.ds(0, SEG)], xsem.at[index])
        rows = pl.ds(pl.multiple_of(index * SEG, SEG), SEG)
        found = dot(classed[...], xb[rows, :]).astype(jnp.bfloat16)
        to_rows = pl.ds(pl.multiple_of(index * 16, 16), 16)
        send1[:, to_rows, :] = found.reshape(SHARDS, 16, WIDTH)
        return 0

    lax.fori_loop(0, SEGS, pack, 0)
    load_c = pltpu.make_async_copy(cot_hbm, xb, csem)
    load_c.start()
    pl.semaphore_wait(barrier, SHARDS - 1 + 2 * (SLIDES - 1))

    def scatter(step, _):
        to = peer(me, step)
        pltpu.make_async_remote_copy(
            src_ref=send1.at[to], dst_ref=recv1.at[step], send_sem=ssem1,
            recv_sem=rsem1.at[lax.div(step, 8)],
            device_id={"seq": to}, device_id_type=MESH,
        ).start()
        return 0

    def tell(step, _):
        to = peer(me, step)
        pltpu.make_async_remote_copy(
            src_ref=dsend, dst_ref=dall.at[step], send_sem=dssem, recv_sem=drsem,
            device_id={"seq": to}, device_id_type=MESH,
        ).start()
        return 0

    lax.fori_loop(1, 8, scatter, 0)
    lax.fori_loop(1, SHARDS, tell, 0)
    pltpu.make_async_copy(dsend, dall.at[0], drsem).start()
    lax.fori_loop(8, SHARDS, scatter, 0)
    pltpu.make_async_copy(send1.at[me], recv1.at[0], rsem1.at[0]).start()

    wait_bytes(dall, drsem)
    target = target_rows(me, jnp.max(dall[...].astype(jnp.float32), axis=1))

    def build(part, _):
        rows = iota((SEG, ROWS), 0) + part * SEG
        place[part] = one_hot(rows == target)
        return 0

    lax.fori_loop(0, SEGS, build, 0)
    ordered[...] = one_hot(col == 32 * (row % RATE) + 16 * (row % STRIDE // RATE) + row // STRIDE)
    load_c.wait()

    def class_order(part, _):
        rows = pl.ds(pl.multiple_of(part * SEG, SEG), SEG)
        xb[rows, :] = dot(classed[...], xb[rows, :]).astype(jnp.bfloat16)
        return 0

    lax.fori_loop(0, SEGS, class_order, 0)
    load_w.wait()
    pair_at = lax.div(head, 2) * 128
    for part in range(3):
        at = pl.multiple_of(jnp.minimum(pair_at, WIDTH - 128) + part * WIDTH, 128)
        wfar[:, part * 128 : (part + 1) * 128] = wqkv[:, pl.ds(at, 128)]

    gathered = recv1.reshape(ROWS, WIDTH)
    gain = gain_ref[...].reshape(1, WIDTH)
    half = lax.rem(head, 2)

    def far_project(group):
        mine = iota((SEG, 128), 1) // HEAD_DIM == half
        rows = slice(group * SEG, group * SEG + SEG)
        out = dot(normalize(gathered[rows, :].astype(jnp.float32), gain), wfar[...])
        out = out.astype(jnp.bfloat16)
        zero, one = jnp.bfloat16(0.0), jnp.bfloat16(1.0)
        qf[rows, :] = jnp.where(mine, out[:, :128] * jnp.bfloat16(score_scale), zero)
        kv[core, 0, rows, :] = out[:, 128:256]
        kv[core, 1, rows, :] = jnp.where(mine, out[:, 256:], one)

    def swap(stage):
        rows = pl.ds(stage * 3 * SEG, 3 * SEG if stage == 0 else SEG)
        return pltpu.make_async_remote_copy(
            src_ref=kv.at[core, :, rows], dst_ref=kv.at[core, :, rows],
            send_sem=kvs.at[stage], recv_sem=kvr.at[stage],
            device_id={"seq": mate}, device_id_type=MESH,
        )

    blocks = [(side, slice(at, at + SEG)) for side in range(2) for at in range(0, ROWS, SEG)]

    def far_blocks(queries):
        accum = peak = None
        upcoming = dot_t(queries, kv[blocks[0][0], 0, blocks[0][1], :])
        for number, (side, keys) in enumerate(blocks):
            scores = upcoming
            if number + 1 < len(blocks):
                after, cut = blocks[number + 1]
                upcoming = dot_t(queries, kv[after, 0, cut, :])
            top = jnp.max(scores, axis=-1, keepdims=True)
            if peak is not None:
                top = jnp.maximum(peak, top)
                accum = accum * jnp.exp(peak - top)
            term = dot(jnp.exp(scores - top).astype(jnp.bfloat16), kv[side, 1, keys, :])
            accum = term if accum is None else accum + term
            peak = top
        return accum, peak

    def far_result(accum, peak):
        lane = iota((SEG, 128), 1)
        mine = lane // HEAD_DIM == half
        mixed = accum / pltpu.roll(accum, 64, 1)
        level = peak + jnp.log(jnp.where(mine, 1.0, accum))
        high = level.astype(jnp.bfloat16).astype(jnp.float32)
        tail = jnp.where(lane % 64 < 32, high, level - high)
        return jnp.where(mine, mixed, tail).astype(jnp.bfloat16)

    def moved(part, group):
        rows = slice(group * SEG, group * SEG + SEG)
        found = dot(place[part, :, rows], gathered[rows, :]).astype(jnp.bfloat16)
        return found.reshape(SHARDS, 16, WIDTH)

    for group in range(SEGS - 1):
        wait_bytes(recv1.at[pl.ds(8 * group, 8)], rsem1.at[group])

        def regroup(part, _, group=group):
            term = moved(part, group)
            send2[part] = term if group == 0 else send2[part] + term
            return 0

        @pl.when(head < HEADS)
        def _(group=group):
            far_project(group)
            if group == SEGS - 2:
                swap(0).start()

        lax.fori_loop(0, SEGS, regroup, 0)

    def deliver(part, _):
        send2[part] = send2[part] + moved(part, SEGS - 1)

        def give(step, _):
            to = peer(me, step)
            pltpu.make_async_remote_copy(
                src_ref=send2.at[part, to], dst_ref=recv2.at[part, me],
                send_sem=ssem2.at[part], recv_sem=rsem2.at[part],
                device_id={"seq": to}, device_id_type=MESH,
            ).start()
            return 0

        lax.fori_loop(1, SHARDS, give, 0)
        pltpu.make_async_copy(send2.at[part, me], recv2.at[part, me], rsem2.at[part]).start()
        return 0

    wait_bytes(recv1.at[pl.ds(24, 8)], rsem1.at[SEGS - 1])

    def far(index, _):
        rows = pl.ds(pl.multiple_of(index * SEG, SEG), SEG)
        fout[rows, :] = far_result(*far_blocks(qf[rows, :]))
        return 0

    def return_far():
        def reorder(part, _):
            farsend[part] = dot(place[part], fout[...]).astype(jnp.bfloat16).reshape(
                SHARDS, 16, 128
            )
            return 0

        lax.fori_loop(0, SEGS, reorder, 0)

        def give_far(step, _):
            to = peer(me, step)
            pltpu.make_async_remote_copy(
                src_ref=farsend.at[:, to], dst_ref=farrecv.at[me], send_sem=fss, recv_sem=frs,
                device_id={"seq": to}, device_id_type=MESH,
            ).start()
            return 0

        lax.fori_loop(1, SHARDS, give_far, 0)
        pltpu.make_async_copy(farsend.at[:, me], farrecv.at[me], frs).start()

    def deliver_beside_far(part, _):
        deliver(part, 0)

        @pl.when(jnp.logical_and(head < HEADS, part == 0))
        def _():
            far_project(SEGS - 1)
            swap(1).start()

        @pl.when(jnp.logical_and(head < HEADS, jnp.logical_or(part == 1, part == 2)))
        def _():
            @pl.when(part == 1)
            def _():
                swap(0).wait()
                swap(1).wait()

            lax.fori_loop(2 * part - 2, 2 * part, far, 0)
            pl.when(part == 2)(return_far)

        return 0

    lax.fori_loop(0, SEGS, deliver_beside_far, 0)
    load_o.wait()
    low = iota((SEG, 128), 1) < HEAD_DIM
    low_far = iota((16, 128), 1) < HEAD_DIM

    wait_bytes(send1.at[pl.ds(0, SHARDS - 1)], ssem1)
    attn = send1.reshape(ROWS, WIDTH)
    encst = recv1.reshape(ROWS, WIDTH)

    def near_level(part):
        slot = lax.rem(part, 2)
        wait_bytes(recv2.at[part], rsem2.at[part])
        for at in range(0, SHARDS, 8):
            rows = recv2[part, at : at + 8].reshape(128, WIDTH).astype(jnp.float32)
            normed[16 * at : 16 * at + 128, :] = normalize(rows, gain)

        def project(index):
            for kind in range(3):
                cols = slice(kind * WIDTH + index * 256, kind * WIDTH + index * 256 + 256)
                qkv[:, cols] = dot(normed[...], wqkv[:, cols]).astype(jnp.bfloat16)

        def operands(number):
            pair, side = number // 2, number % 2
            mine = low if side == 0 else jnp.logical_not(low)
            queries = qkv[:, lanes(pair)] * jnp.bfloat16(score_scale)
            values = qkv[:, lanes(pair + 2 * PAIRS)]
            return (
                jnp.where(mine, queries, jnp.zeros_like(queries)),
                qkv[:, lanes(pair + PAIRS)],
                jnp.where(mine, values, jnp.ones_like(values)),
            )

        def start_head(number):
            queries, keys, values = operands(number)
            return dot_t(queries, keys), values

        project(0)
        upcoming = start_head(0)
        kept = []
        for number in range(HEADS):
            scores, values = upcoming
            if number % 4 == 0 and number + 4 < HEADS:
                project(number // 4 + 1)
            if number + 1 < HEADS:
                upcoming = start_head(number + 1)
            peak = jnp.max(scores, axis=-1, keepdims=True)
            weights = jnp.exp(scores - peak).astype(jnp.bfloat16)
            kept.append((dot(weights, values), peak))
            if number % 2:
                (accum0, peak0), (accum1, peak1) = kept
                kept = []
                total = pltpu.roll(jnp.where(low, accum1, accum0), 64, 1)
                pair = number // 2
                mix[slot, pair] = jnp.where(low, accum0, accum1) / total
                lse[slot, pair] = jnp.where(low, peak0, peak1) + jnp.log(total)

    def merge(part):
        slot = lax.rem(part, 2)
        for src in range(FAR_OWNERS):
            number = src // 2
            pair, half = number // 2, number % 2
            rows = slice(16 * src, 16 * src + 16)
            near_part = mix[slot, pair, rows, :]
            near_lse = lse[slot, pair, rows, :]
            far_part = farrecv[src, part].astype(jnp.float32)
            other = HEAD_DIM * (1 - half)
            far_lse = far_part[:, other : other + 1] + far_part[:, other + 32 : other + 33]
            top = jnp.maximum(near_lse, far_lse)
            near_share = jnp.exp(near_lse - top)
            far_share = jnp.exp(far_lse - top)
            mixed = (near_share * near_part + far_share * far_part) / (near_share + far_share)
            mine = low_far if half == 0 else jnp.logical_not(low_far)
            mix[slot, pair, rows, :] = jnp.where(mine, mixed, near_part)

        here = pl.ds(pl.multiple_of(part * SEG, SEG), SEG)
        for group in range(GROUPS):
            attn[here, lanes(group)] = mix[slot, group].astype(jnp.bfloat16)
        for index in range(3):
            cols = slice(index * 256, index * 256 + 256)
            term = lax.dot_general(
                attn[here, :], xb[here, cols], (((0,), (0,)), ((), ())),
                preferred_element_type=jnp.float32,
            )
            for sub in range(2):
                group = 2 * index + sub
                piece = term[:, lanes(sub)]
                grad[group] = jnp.where(part == 0, piece, grad[group] + piece)

    def segment(step, _):
        pl.when(step < SEGS)(functools.partial(near_level, step))

        @pl.when(step == 1)
        def _():
            wait_bytes(farrecv, frs)

        pl.when(step > 0)(functools.partial(merge, step - 1))
        return 0

    def finish(part, _):
        here = pl.ds(pl.multiple_of(part * SEG, SEG), SEG)
        inputs = recv2[part].reshape(SEG, WIDTH)
        for index in range(3):
            cols = slice(index * 256, index * 256 + 256)
            projected = dot(attn[here, :], wout[:, cols])
            summed = (inputs[:, cols].astype(jnp.float32) + projected).astype(jnp.bfloat16)
            encst[here, cols] = dot(ordered[...], summed).astype(jnp.bfloat16)
        pltpu.make_async_copy(encst.at[here], enc_hbm.at[here], esem.at[part]).start()
        return 0

    lax.fori_loop(0, SEGS + 1, segment, 0)

    def cast_grad(side):
        for group in range(3):
            gsend[side, :, lanes(group)] = grad[3 * side + group].astype(jnp.bfloat16)

    cast_grad(1 - core)
    join = pltpu.make_async_remote_copy(
        src_ref=gsend.at[1 - core], dst_ref=gmate, send_sem=jss, recv_sem=jrs,
        device_id={"seq": mate}, device_id_type=MESH,
    )
    join.start()
    cast_grad(core)
    finish(0, 0)
    join.wait()
    both = gsend[core].astype(jnp.float32) + gmate[...].astype(jnp.float32)
    gpart[...] = both.astype(jnp.bfloat16).reshape(SHARDS // 2, 48, 384)

    def give_grad(step, _):
        to = lax.rem(lax.div(me, 8) + lax.rem(step, 4), 4) * 8 + lax.rem(
            lax.rem(lax.div(me, 2), 4) + lax.rem(step + lax.div(step, 4), 4), 4
        ) * 2 + core
        pltpu.make_async_remote_copy(
            src_ref=gpart.at[lax.div(to, 2)], dst_ref=grecv.at[head], send_sem=gss, recv_sem=grs,
            device_id={"seq": to}, device_id_type=MESH,
        ).start()
        return 0

    lax.fori_loop(1, SHARDS // 2, give_grad, 0)
    pltpu.make_async_copy(gpart.at[head], grecv.at[head], grs).start()
    lax.fori_loop(1, SEGS, finish, 0)
    wait_bytes(grecv, grs)
    summed = jnp.sum(grecv[...].astype(jnp.float32), axis=0)
    ysend[0] = summed[:24]
    ysend[1] = summed[24:]
    for step in range(SLIDES):
        for across in range(2):
            side = lax.rem(core + across, 2)
            landing = yrecv.at[core, dp]
            if step or across:
                pltpu.make_async_remote_copy(
                    src_ref=ysend.at[side], dst_ref=landing, send_sem=yss, recv_sem=yrs,
                    device_id={"dp": lax.rem(dp + step, SLIDES), "seq": me - core + side},
                    device_id_type=MESH,
                ).start()
            else:
                pltpu.make_async_copy(ysend.at[side], landing, yrs).start()
    wait_bytes(yrecv, yrs)
    for side in range(2):
        total = (yrecv[side, 0] + yrecv[side, 1]) + (yrecv[side, 2] + yrecv[side, 3])
        grad_ref[:, 384 * side : 384 * side + 384] = total

    wait_bytes(dall.at[pl.ds(0, SHARDS - 1)], dssem)
    for part in range(SEGS):
        wait_bytes(send2.at[part, pl.ds(0, SHARDS - 1)], ssem2.at[part])
        wait_bytes(encst.at[pl.ds(part * SEG, SEG)], esem.at[part])

    @pl.when(head < HEADS)
    def _():
        wait_bytes(farsend.at[:, pl.ds(0, SHARDS - 1)], fss)

    wait_bytes(gpart.at[pl.ds(0, SHARDS // 2 - 1)], gss)
    wait_bytes(yrecv.at[0], yss)
    wait_bytes(yrecv.at[1, pl.ds(0, SLIDES - 1)], yss)


def hand_on(src, dst, held, in_sems, out_sems):
    pieces = [pl.ds(at, SEG) for at in range(0, ROWS, SEG)]
    into = [
        pltpu.make_async_copy(src.at[rows], held.at[rows], in_sems.at[number])
        for number, rows in enumerate(pieces)
    ]
    out = [
        pltpu.make_async_copy(held.at[rows], dst.at[rows], out_sems.at[number])
        for number, rows in enumerate(pieces)
    ]
    for copy in into:
        copy.start()
    for first, second in zip(into, out):
        first.wait()
        second.start()
    for copy in out:
        copy.wait()


def body(tile_rows, block_dest, norm_gain, qkv_weight, out_weight, cotangent):
    bf16, f32 = jnp.bfloat16, jnp.float32
    dma = pltpu.SemaphoreType.DMA
    anywhere = pl.BlockSpec(memory_space=pl.ANY)
    vmem = pl.BlockSpec(memory_space=pltpu.VMEM)
    encoded, grad = pl.pallas_call(
        kernel,
        out_shape=(
            jax.ShapeDtypeStruct((ROWS, WIDTH), bf16),
            jax.ShapeDtypeStruct((24, WIDTH), f32),
        ),
        in_specs=[anywhere, vmem, vmem, anywhere, anywhere, anywhere],
        out_specs=(anywhere, vmem),
        scratch_shapes=[
            pltpu.VMEM((ROWS, WIDTH), bf16),
            pltpu.VMEM((SHARDS, 64, WIDTH), bf16),
            pltpu.VMEM((SHARDS, 64, WIDTH), bf16),
            pltpu.VMEM((8, 128), jnp.int32),
            pltpu.VMEM((SHARDS, 8, 128), jnp.int32),
            pltpu.VMEM((SEGS, SHARDS, 16, WIDTH), bf16),
            pltpu.VMEM((SEGS, SHARDS, 16, WIDTH), bf16),
            pltpu.VMEM((SEGS, SEG, ROWS), bf16),
            pltpu.VMEM((SEG, SEG), bf16),
            pltpu.VMEM((SEG, SEG), bf16),
            pltpu.VMEM((2, 2, ROWS, 128), bf16),
            pltpu.VMEM((ROWS, 128), bf16),
            pltpu.VMEM((ROWS, 128), bf16),
            pltpu.VMEM((SEGS, SHARDS, 16, 128), bf16),
            pltpu.VMEM((FAR_OWNERS, SEGS, 16, 128), bf16),
            pltpu.VMEM((WIDTH, 3 * WIDTH), bf16),
            pltpu.VMEM((WIDTH, 384), bf16),
            pltpu.VMEM((WIDTH, WIDTH), bf16),
            pltpu.VMEM((SEG, WIDTH), bf16),
            pltpu.VMEM((SEG, 3 * WIDTH), bf16),
            pltpu.VMEM((2, PAIRS, SEG, 128), f32),
            pltpu.VMEM((2, PAIRS, SEG, 128), f32),
            pltpu.VMEM((GROUPS, WIDTH, 128), f32),
            pltpu.VMEM((2, WIDTH, 384), bf16),
            pltpu.VMEM((WIDTH, 384), bf16),
            pltpu.VMEM((SHARDS // 2, 48, 384), bf16),
            pltpu.VMEM((SHARDS // 2, 48, 384), bf16),
            pltpu.VMEM((2, 24, 384), f32),
            pltpu.VMEM((2, SLIDES, 24, 384), f32),
            dma, dma((SEGS,)), dma, dma, dma((SEGS,)), dma((SEGS,)), dma((2,)), dma((2,)),
            dma, dma, dma, dma, dma, dma, dma, dma,
            dma((SEGS,)), dma, dma, dma, dma((SEGS,)),
        ],
        compiler_params=pltpu.CompilerParams(
            collective_id=0, has_side_effects=True, vmem_limit_bytes=62 * 1024 * 1024
        ),
        name="slide_layer",
    )(
        tile_rows.reshape(ROWS, WIDTH), block_dest, norm_gain,
        qkv_weight, out_weight, cotangent.reshape(ROWS, WIDTH),
    )
    encoded = pl.pallas_call(
        hand_on,
        out_shape=jax.ShapeDtypeStruct((ROWS, WIDTH), bf16),
        in_specs=[anywhere],
        out_specs=anywhere,
        scratch_shapes=[pltpu.VMEM((ROWS, WIDTH), bf16), dma((SEGS,)), dma((SEGS,))],
        name="hand_on",
    )(encoded)
    return encoded.reshape(1, ROWS, WIDTH), grad


def solution(mesh):
    return jax.shard_map(
        body,
        mesh=mesh,
        in_specs=(P("dp", "seq", None), P("dp", "seq"), P(), P(), P(), P("dp", "seq", None)),
        out_specs=(P("dp", "seq", None), P("seq", None)),
        check_vma=False,
    )
```
